512 devices in a mesh: row: 16 (over x, z_lo, core), col: 32 (over y, z_hi).
Axes of the slice: x: 4, y: 8, z: 8 (z_hi: 4, z_lo: 2; z = z_hi * 2 + z_lo), core: 2. Of those that a mesh axis runs over, the one named last changes fastest.
Arguments:
- features: float32 [65536, 256], P(('row', 'col')), may hold values from -6 to 6
- adjacency_tiles: float32 [32768, 128, 128], P(('row', 'col')), may hold values from -0.0625 to 0.0625
- tile_rows: int32 [32768], P(('row', 'col')), may hold values from 0 to 31
- tile_cols: int32 [32768], P(('row', 'col')), may hold values from 0 to 15
- tile_count: int32 [512], P(('row', 'col')), may hold values from 8 to 64, as said below
- weight: float32 [256, 256], replicated, may hold values from -0.375 to 0.375
- cotangent: float32 [65536, 256], P(('row', 'col')), may hold values from -0.0234375 to 0.0234375
Outputs:
- activated: float32 [65536, 256], P(('row', 'col'))
- weight_grad: float32 [256, 256], replicated
The draws below stay inside these ranges and needn't reach their ends.
Inputs may be any that keep to these rules, and one draw needn't show every extreme that they name: `tile_count`: some device has all 64 slots live and some other has 8; the rest are skewed toward few live slots.
All inputs are finite; a program needn't handle non-finite values.
Results may differ from the reference program's by a relative error of at most 0.0003.
Values sent between devices are 32-bit elements; how exact they have to be, the bound alone decides.
No kernel may reach another device: no remote copies, remote signals or barrier semaphores. Data moves between devices by JAX's collectives and lax.ppermute only.
A program may use at most 64 MiB of HBM per device.

```python
import jax
import jax.numpy as jnp
from jax import lax

F = 256
TILE = 128
ND = 128
MAXT = 64
GRID = 512
NODES = 65536
TROWS = 32
TCOLS = 16
SLOTS = 32768
N_ROW = 16
N_COL = 32


def draw_tile_count(key, part):
    key = jax.random.fold_in(key, 7)
    first, second, third = jax.random.split(key, 3)
    lowest = MAXT // 8
    levels = 64
    picks = jax.random.randint(first, (GRID,), 0, levels)
    counts = lowest + picks * picks * (MAXT - lowest) // ((levels - 1) * (levels - 1))
    full_dev = jax.random.randint(second, (), 0, GRID)
    small_dev = (full_dev + 1 + jax.random.randint(third, (), 0, GRID - 1)) % GRID
    position = jnp.arange(GRID)
    counts = jnp.where(position == full_dev, MAXT, counts)
    counts = jnp.where(position == small_dev, lowest, counts)
    return counts.astype(jnp.int32)


def set_ends(result, rng, least, largest):
    place = [jax.random.randint(jax.random.fold_in(rng, axis), (), 0, length) for axis, length in enumerate(result.shape)]
    widest = result.shape.index(max(result.shape))
    next_to = place[:widest] + [(place[widest] + 1) % result.shape[widest]] + place[widest + 1:]
    return result.at[tuple(place)].set(least).at[tuple(next_to)].set(largest)


def level_of(stream_key, extent, pieces, least, high):
    def one(dim, shards_of):
        heights = jax.random.uniform(jax.random.fold_in(jax.random.fold_in(stream_key, 6), dim), (shards_of,), jnp.float32, least / len(pieces), high / len(pieces))
        return jnp.repeat(jnp.exp(heights), extent[dim] // shards_of).reshape((-1,) + (1,) * (len(extent) - dim - 1))

    gain = one(*pieces[0])
    for cut in pieces[1:]:
        gain = gain * one(*cut)
    return gain


def bell_draw(own_key, dims, deviation, most, pieces=(), kind=jnp.bfloat16):
    values = jax.random.normal(own_key, dims, jnp.float32) * deviation
    if len(pieces) > 0:
        values = level_of(own_key, dims, pieces, -0.22, 0.18) * values
    return jnp.clip(values, min=-most, max=most).astype(kind)


def setup_inputs(seed: int = 0) -> dict:
    seeds = jax.random.split(jax.random.key(seed), 8)
    features = bell_draw(seeds[0], (NODES, F), 1.0, 6.0, ((0, 512),), jnp.float32)
    adjacency_tiles = bell_draw(seeds[1], (SLOTS, TILE, TILE), (TILE * MAXT) ** -0.5, 0.0625, ((0, 512),), jnp.float32)
    tile_rows = set_ends(jax.random.randint(seeds[2], (SLOTS,), 0, TROWS), jax.random.fold_in(seeds[2], 1), 0, TROWS - 1).astype(jnp.int32)
    tile_cols = set_ends(jax.random.randint(seeds[3], (SLOTS,), 0, TCOLS), jax.random.fold_in(seeds[3], 1), 0, TCOLS - 1).astype(jnp.int32)
    tile_count = draw_tile_count(jax.random.fold_in(seeds[7], 71), 0)
    weight = bell_draw(seeds[5], (F, F), F ** -0.5, 0.375, (), jnp.float32)
    cotangent = bell_draw(seeds[6], (NODES, F), (1.0 / 256), 0.0234375, ((0, 512),), jnp.float32)
    return {"features": features, "adjacency_tiles": adjacency_tiles, "tile_rows": tile_rows, "tile_cols": tile_cols, "tile_count": tile_count, "weight": weight, "cotangent": cotangent}


root_two_pi = 0.7978845608028654
cubic = 0.044715


def gelu_parts(z):
    inner = root_two_pi * (z + cubic * z * z * z)
    slope_t = jnp.tanh(inner)
    value = 0.5 * z * (1.0 + slope_t)
    slope = 0.5 * (1.0 + slope_t) + 0.5 * z * (1.0 - slope_t * slope_t) * root_two_pi * (1.0 + 3.0 * cubic * z * z)
    return value, slope


def reference(features, adjacency_tiles, tile_rows, tile_cols, tile_count, weight, cotangent):
    highest = lax.Precision.HIGHEST
    grid_feat = features.reshape(N_ROW, N_COL, ND, F)
    tiles = adjacency_tiles.reshape(N_ROW * N_COL, MAXT, TILE, TILE)
    row_ids = tile_rows.reshape(N_ROW * N_COL, MAXT)
    col_ids = tile_cols.reshape(N_ROW * N_COL, MAXT)

    def device(carry, inputs):
        index, tile_block, rows_here, cols_here, count = inputs
        grid_row = index // N_COL
        grid_col = index % N_COL
        column = lax.dynamic_index_in_dim(grid_feat, grid_col, 1, keepdims=False)
        blocks = column.reshape(TCOLS, TILE, F)
        chosen = blocks[cols_here]
        prods = jnp.einsum("sij,sjf->sif", tile_block, chosen, precision=highest)
        live = (jnp.arange(MAXT, dtype=jnp.int32) < count).astype(jnp.float32)
        selector = (rows_here[None, :] == jnp.arange(TROWS, dtype=jnp.int32)[:, None]).astype(jnp.float32) * live[None, :]
        partial_value = jnp.dot(selector, prods.reshape(MAXT, TILE * F), precision=highest).reshape(N_COL * ND, F)
        current = lax.dynamic_index_in_dim(carry, grid_row, 0, keepdims=False)
        carry = lax.dynamic_update_index_in_dim(carry, current + partial_value, grid_row, 0)
        return carry, None

    start = jnp.zeros((N_ROW, N_COL * ND, F), jnp.float32)
    indices = jnp.arange(N_ROW * N_COL, dtype=jnp.int32)
    summed, _ = lax.scan(device, start, (indices, tiles, row_ids, col_ids, tile_count))
    aggregated = summed.reshape(NODES, F)
    pre = jnp.dot(aggregated, weight, precision=highest)
    activated, slope = gelu_parts(pre)
    grad_pre = cotangent * slope
    weight_grad = jnp.dot(aggregated.T, grad_pre, precision=highest)
    return activated, weight_grad
```

```python
import functools

import jax
import jax.numpy as jnp
from jax import lax
from jax.experimental import pallas as pl
from jax.experimental.pallas import tpu as pltpu
from jax.sharding import Mesh, PartitionSpec as P

root_two_pi = 0.7978845608028654
cubic = 0.044715

AXES = ("x", "zl", "c", "yh", "yl", "zh")
SIZES = (4, 2, 2, 4, 2, 4)
NX, NZL, NC, _, _, NZH = SIZES
RING = ("yh", "yl")
NY = 8
ROUNDS = NY // 2
LANES = 128
GROUP = 4
NEAR = ("x", "zl", "c", "yl")
FAR = ("yh", "zh")
NEAR_SIZE = 32


def halves(v):
    high = v.astype(jnp.bfloat16)
    return high, (v - high.astype(jnp.float32)).astype(jnp.bfloat16)


def dot3(a, b, dims):
    ah, al = halves(a)
    bh, bl = halves(b)

    def one(u, v):
        return lax.dot_general(u, v, (dims, ((), ())), preferred_element_type=jnp.float32)

    return one(ah, bh) + (one(al, bh) + one(ah, bl))


def gelu_parts(z):
    inner = root_two_pi * (z + cubic * z * z * z)
    slope_t = jnp.tanh(inner)
    value = 0.5 * z * (1.0 + slope_t)
    slope = 0.5 * (1.0 + slope_t) + 0.5 * z * (1.0 - slope_t * slope_t) * root_two_pi * (
        1.0 + 3.0 * cubic * z * z
    )
    return (value, slope)


def trade(v, axis, way):
    n = lax.axis_size(axis)
    return lax.ppermute(v, axis, [(k, (k + 1 - 2 * ((k + way) % 2)) % n) for k in range(n)])


def ahead(place, axis):
    n = lax.axis_size(axis)
    me = lax.axis_index(axis)
    return lax.rem((1 - 2 * (me % 2)) * (place - me) + n, n)


def swap(v, axes):
    return lax.all_to_all(v, axes, split_axis=0, concat_axis=0, tiled=True)


def share(v, axes):
    return swap(jnp.broadcast_to(v[None], (lax.axis_size(axes),) + v.shape), axes)


def slot_plan(tile_rows, tile_cols, tile_count):
    ids = jnp.arange(tile_rows.shape[0], dtype=jnp.int32)
    place = ahead(tile_rows // NZH, RING) * NZH + ahead(tile_rows % NZH, "zh")
    place = jnp.where(ids < tile_count[0], place, NY * NZH)
    core = lax.rem(tile_cols % NC + lax.axis_index("c"), NC)
    return place * 16 + core * (NX * NZL) + tile_cols // NC


def split_kernel(tiles_ref, out_ref):
    for k in range(tiles_ref.shape[0]):
        out_ref[k] = jnp.concatenate(halves(tiles_ref[k]), axis=1)


def split_tiles(tiles):
    slots, tile, _ = tiles.shape
    step = 8
    return pl.pallas_call(
        split_kernel,
        grid=(slots // step,),
        out_shape=jax.ShapeDtypeStruct((slots, tile, 2 * tile), jnp.bfloat16),
        in_specs=[pl.BlockSpec((step, tile, tile), lambda k: (k, 0, 0))],
        out_specs=pl.BlockSpec((step, tile, 2 * tile), lambda k: (k, 0, 0)),
        compiler_params=pltpu.CompilerParams(vmem_limit_bytes=8 * 1024 * 1024),
        cost_estimate=pl.CostEstimate(flops=4 * 10**6, bytes_accessed=8 * 2**20, transcendentals=0),
    )(tiles)


def product_kernel(half, count_ref, plan_ref, left_ref, own_ref, other_ref, out_ref, pairs):
    blocks = own_ref.shape[0]
    lanes = slice(half * LANES, (half + 1) * LANES)
    for k, source in enumerate((own_ref, other_ref)):
        for b in range(blocks):
            pairs[k * blocks + b] = jnp.concatenate(halves(source[b, :, lanes]), axis=1)
    out_ref[...] = jnp.zeros_like(out_ref)

    @pl.loop(0, (count_ref[0] + GROUP - 1) // GROUP)
    def _(step):
        values = []
        for k in range(GROUP):
            slot = step * GROUP + k
            plan = plan_ref[slot]
            pair = pairs[plan % 16]
            value = jnp.dot(
                left_ref[slot],
                jnp.concatenate([pair, pair], axis=0),
                preferred_element_type=jnp.float32,
            )
            values.append((plan // 16, value[:, :LANES] + value[:, LANES:]))
        for place, value in values:
            out_ref[place] += value


def products(half, count, plan, left, own, other):
    slots, tile, _ = left.shape
    smem = pl.BlockSpec(memory_space=pltpu.SMEM)
    vmem = pl.BlockSpec(memory_space=pltpu.VMEM)
    return pl.pallas_call(
        functools.partial(product_kernel, half),
        out_shape=jax.ShapeDtypeStruct((NY * NZH + 1, tile, LANES), jnp.float32),
        in_specs=[smem, smem, vmem, vmem, vmem],
        out_specs=vmem,
        scratch_shapes=[pltpu.VMEM((NX * NZL * NC, tile, 2 * LANES), jnp.bfloat16)],
        compiler_params=pltpu.CompilerParams(vmem_limit_bytes=20 * 1024 * 1024),
        cost_estimate=pl.CostEstimate(
            flops=8 * slots * tile * tile * LANES, bytes_accessed=8 * 2**20, transcendentals=0
        ),
    )(count, plan, left, own, other)


def node_kernel(*refs):
    *terms, weight_ref, cot_ref, act_ref, grad_ref = refs
    agg = jnp.concatenate([(t[0][...] + t[1][...]) + t[2][...] for t in (terms[:3], terms[3:])], axis=1)
    pre = dot3(agg, weight_ref[...], ((1,), (0,)))
    value, slope = gelu_parts(pre)
    act_ref[...] = value
    grad = dot3(agg, cot_ref[...] * slope, ((0,), (0,)))
    rows = grad.shape[0] // NEAR_SIZE
    for r in range(NEAR_SIZE):
        for h in range(2):
            grad_ref[r, h] = grad[rows * r : rows * (r + 1), h * LANES : (h + 1) * LANES]


def node_step(terms, weight, cotangent):
    vmem = pl.BlockSpec(memory_space=pltpu.VMEM)
    return pl.pallas_call(
        node_kernel,
        out_shape=(
            jax.ShapeDtypeStruct(cotangent.shape, jnp.float32),
            jax.ShapeDtypeStruct((NEAR_SIZE, 2, weight.shape[0] // NEAR_SIZE, LANES), jnp.float32),
        ),
        in_specs=[vmem] * (len(terms) + 2),
        out_specs=(vmem, vmem),
        compiler_params=pltpu.CompilerParams(vmem_limit_bytes=8 * 1024 * 1024),
    )(*terms, weight, cotangent)


def after(values, witness):
    here = lax.optimization_barrier((*(v for v in values if v is not None), witness))
    return [None if v is None else here[sum(u is not None for u in values[:k])] for k, v in enumerate(values)]


def chunk(sums, ahead):
    return sums[ahead * NZH : (ahead + 1) * NZH]


def advance(sums, step, got):
    pair = [chunk(sums, ROUNDS - step), chunk(sums, (ROUNDS + step) % NY)]
    if step == ROUNDS:
        return pair[0] + (got[0] + got[1])
    return [v if g is None else v + g for v, g in zip(pair, got[::-1])]


def send(pair):
    return trade(pair[0], RING, 0), trade(pair[1], RING, 1)


def spread(own, first):
    got = trade(own[2], "zh", first)
    direct = trade(own[1 + 2 * first], "zh", first)
    return own[0], direct, trade(own[3 - 2 * first] + got, "zh", 1 - first)


def body(features, adjacency_tiles, tile_rows, tile_cols, tile_count, weight, cotangent):
    plan = slot_plan(tile_rows, tile_cols, tile_count)
    own = share(features, ("x", "zl"))
    other = lax.ppermute(own, "c", [(0, 1), (1, 0)])
    arrays = (tile_count, plan, split_tiles(adjacency_tiles), own, other)
    sums_a = products(0, *arrays)
    out_a = chunk(sums_a, ROUNDS)
    got_a = (trade(out_a, RING, 0), None)
    sums_b = products(1, *arrays)
    out_b = [chunk(sums_b, ROUNDS)]
    got_b = (None, trade(out_b[0], RING, 1))
    for step in range(1, ROUNDS):
        out_a = advance(sums_a, step, after(got_a, out_b[0]))
        got_a = send(out_a)
        out_b = advance(sums_b, step, after(got_b, out_a[0]))
        got_b = send(out_b)
    last_a = advance(sums_a, ROUNDS, after(got_a, out_b[0]))
    terms = spread(last_a, 0)
    last_b = advance(sums_b, ROUNDS, after(got_b, last_a))
    terms += spread(last_b, 1)
    activated, grad = node_step(terms, weight, cotangent)
    grad = jnp.sum(swap(grad, NEAR), axis=0)
    grad = jnp.sum(share(grad, FAR), axis=0)
    grad = share(grad, NEAR)
    width = weight.shape[0]
    weight_grad = grad.swapaxes(1, 2).reshape(width, width)
    return (activated, weight_grad)


def solution(mesh):
    split = Mesh(mesh.devices.reshape(SIZES), AXES)
    placed = (P(AXES, None), P(AXES, None, None), P(AXES), P(AXES), P(AXES), P(), P(AXES, None))
    return jax.shard_map(
        body, mesh=split, in_specs=placed, out_specs=(P(AXES, None), P()), check_vma=False
    )
```

```python
import functools

import jax
import jax.numpy as jnp
from jax import lax
from jax.experimental import pallas as pl
from jax.experimental.pallas import tpu as pltpu
from jax.sharding import Mesh, PartitionSpec as P

root_two_pi = 0.7978845608028654
cubic = 0.044715

AXES = ("x", "zl", "c", "yh", "yl", "zh")
SIZES = (4, 2, 2, 4, 2, 4)
NX, NZL, NC, _, _, NZH = SIZES
RING = ("yh", "yl")
NY = 8
ROUNDS = NY // 2
LANES = 128
GROUP = 4
NEAR = ("x", "zl", "c", "yl")
FAR = ("yh", "zh")
NEAR_SIZE = 32


def halves(v):
    high = v.astype(jnp.bfloat16)
    return high, (v - high.astype(jnp.float32)).astype(jnp.bfloat16)


def dot3(a, b, dims):
    ah, al = halves(a)
    bh, bl = halves(b)

    def one(u, v):
        return lax.dot_general(u, v, (dims, ((), ())), preferred_element_type=jnp.float32)

    return one(ah, bh) + (one(al, bh) + one(ah, bl))


def gelu_parts(z):
    inner = root_two_pi * (z + cubic * z * z * z)
    slope_t = jnp.tanh(inner)
    value = 0.5 * z * (1.0 + slope_t)
    slope = 0.5 * (1.0 + slope_t) + 0.5 * z * (1.0 - slope_t * slope_t) * root_two_pi * (
        1.0 + 3.0 * cubic * z * z
    )
    return (value, slope)


def trade(v, axis, way):
    n = lax.axis_size(axis)
    return lax.ppermute(v, axis, [(k, (k + 1 - 2 * ((k + way) % 2)) % n) for k in range(n)])


def ahead(place, axis):
    n = lax.axis_size(axis)
    me = lax.axis_index(axis)
    return lax.rem((1 - 2 * (me % 2)) * (place - me) + n, n)


def swap(v, axes):
    return lax.all_to_all(v, axes, split_axis=0, concat_axis=0, tiled=True)


def share(v, axes):
    return swap(jnp.broadcast_to(v[None], (lax.axis_size(axes),) + v.shape), axes)


def slot_plan(tile_rows, tile_cols, tile_count):
    ids = jnp.arange(tile_rows.shape[0], dtype=jnp.int32)
    place = ahead(tile_rows // NZH, RING) * NZH + tile_rows % NZH
    place = jnp.where(ids < tile_count[0], place, NY * NZH)
    core = lax.rem(tile_cols % NC + lax.axis_index("c"), NC)
    return place * 16 + core * (NX * NZL) + tile_cols // NC


def split_kernel(tiles_ref, out_ref):
    for k in range(tiles_ref.shape[0]):
        out_ref[k] = jnp.concatenate(halves(tiles_ref[k]), axis=1)


def split_tiles(tiles):
    slots, tile, _ = tiles.shape
    step = 8
    return pl.pallas_call(
        split_kernel,
        grid=(slots // step,),
        out_shape=jax.ShapeDtypeStruct((slots, tile, 2 * tile), jnp.bfloat16),
        in_specs=[pl.BlockSpec((step, tile, tile), lambda k: (k, 0, 0))],
        out_specs=pl.BlockSpec((step, tile, 2 * tile), lambda k: (k, 0, 0)),
        compiler_params=pltpu.CompilerParams(vmem_limit_bytes=8 * 1024 * 1024),
        cost_estimate=pl.CostEstimate(flops=4 * 10**6, bytes_accessed=8 * 2**20, transcendentals=0),
    )(tiles)


def product_kernel(count_ref, plan_ref, left_ref, own_ref, other_ref, out_a_ref, out_b_ref, high, low):
    blocks = own_ref.shape[0]
    for k, source in enumerate((own_ref, other_ref)):
        for b in range(blocks):
            high[k * blocks + b], low[k * blocks + b] = halves(source[b])
    out_a_ref[...] = jnp.zeros_like(out_a_ref)
    out_b_ref[...] = jnp.zeros_like(out_b_ref)

    @pl.loop(0, (count_ref[0] + GROUP - 1) // GROUP)
    def _(step):
        for k in range(GROUP):
            slot = step * GROUP + k
            plan = plan_ref[slot]
            left = left_ref[slot]
            right = high[plan % 16]
            value = jnp.dot(
                jnp.concatenate([left, left[:, : left.shape[0]]], axis=1),
                jnp.concatenate([right, right, low[plan % 16]], axis=0),
                preferred_element_type=jnp.float32,
            )
            out_a_ref[plan // 16] += value[:, :LANES]
            out_b_ref[plan // 16] += value[:, LANES:]


def products(count, plan, left, own, other):
    slots, tile, _ = left.shape
    blocks = (2 * own.shape[0], tile, 2 * LANES)
    smem = pl.BlockSpec(memory_space=pltpu.SMEM)
    vmem = pl.BlockSpec(memory_space=pltpu.VMEM)
    return pl.pallas_call(
        product_kernel,
        out_shape=[jax.ShapeDtypeStruct((NY * NZH + 1, tile, LANES), jnp.float32)] * 2,
        in_specs=[smem, smem, vmem, vmem, vmem],
        out_specs=[vmem, vmem],
        scratch_shapes=[pltpu.VMEM(blocks, jnp.bfloat16)] * 2,
        compiler_params=pltpu.CompilerParams(vmem_limit_bytes=20 * 1024 * 1024),
        cost_estimate=pl.CostEstimate(
            flops=12 * slots * tile * tile * LANES, bytes_accessed=8 * 2**20, transcendentals=0
        ),
    )(count, plan, left, own, other)


def node_kernel(terms_ref, weight_ref, cot_ref, act_ref, grad_ref):
    agg = (terms_ref[0] + terms_ref[1]) + (terms_ref[2] + terms_ref[3])
    pre = dot3(agg, weight_ref[...], ((1,), (0,)))
    value, slope = gelu_parts(pre)
    act_ref[...] = value
    grad = dot3(agg, cot_ref[...] * slope, ((0,), (0,)))
    rows = grad.shape[0] // NEAR_SIZE
    for r in range(NEAR_SIZE):
        for h in range(2):
            grad_ref[r, h] = grad[rows * r : rows * (r + 1), h * LANES : (h + 1) * LANES]


def node_step(terms, weight, cotangent):
    vmem = pl.BlockSpec(memory_space=pltpu.VMEM)
    return pl.pallas_call(
        node_kernel,
        out_shape=(
            jax.ShapeDtypeStruct(cotangent.shape, jnp.float32),
            jax.ShapeDtypeStruct((NEAR_SIZE, 2, weight.shape[0] // NEAR_SIZE, LANES), jnp.float32),
        ),
        in_specs=[vmem] * 3,
        out_specs=(vmem, vmem),
        compiler_params=pltpu.CompilerParams(vmem_limit_bytes=8 * 1024 * 1024),
    )(terms, weight, cotangent)


def after(values, witness):
    here = lax.optimization_barrier((*(v for v in values if v is not None), witness))
    return [None if v is None else here[sum(u is not None for u in values[:k])] for k, v in enumerate(values)]


def chunk(sums, ahead):
    return sums[ahead * NZH : (ahead + 1) * NZH]


def advance(sums, step, got):
    pair = [chunk(sums, ROUNDS - step), chunk(sums, (ROUNDS + step) % NY)]
    if step == ROUNDS:
        return pair[0] + (got[0] + got[1])
    return [v if g is None else v + g for v, g in zip(pair, got[::-1])]


def send(pair):
    return trade(pair[0], RING, 0), trade(pair[1], RING, 1)


def body(features, adjacency_tiles, tile_rows, tile_cols, tile_count, weight, cotangent):
    plan = slot_plan(tile_rows, tile_cols, tile_count)
    own = share(features, ("x", "zl"))
    other = lax.ppermute(own, "c", [(0, 1), (1, 0)])
    arrays = (tile_count, plan, split_tiles(adjacency_tiles), own, other)
    sums_a, sums_b = products(*arrays)
    got_a = (None, trade(chunk(sums_a, ROUNDS), RING, 1))
    out_b = [chunk(sums_b, ROUNDS)]
    got_b = (trade(out_b[0], RING, 0), None)
    for step in range(1, ROUNDS):
        out_a = advance(sums_a, step, after(got_a, out_b[0]))
        got_a = send(out_a)
        out_b = advance(sums_b, step, after(got_b, out_a[0]))
        got_b = send(out_b)
    last_a = advance(sums_a, ROUNDS, after(got_a, out_b[0]))
    last_b = advance(sums_b, ROUNDS, after(got_b, last_a))
    terms = swap(jnp.concatenate([last_a, last_b], axis=2), "zh")
    activated, grad = node_step(terms, weight, cotangent)
    grad = jnp.sum(swap(grad, NEAR), axis=0)
    grad = jnp.sum(share(grad, FAR), axis=0)
    grad = share(grad, NEAR)
    width = weight.shape[0]
    weight_grad = grad.swapaxes(1, 2).reshape(width, width)
    return (activated, weight_grad)


def solution(mesh):
    split = Mesh(mesh.devices.reshape(SIZES), AXES)
    placed = (P(AXES, None), P(AXES, None, None), P(AXES), P(AXES), P(AXES), P(), P(AXES, None))
    return jax.shard_map(
        body, mesh=split, in_specs=placed, out_specs=(P(AXES, None), P()), check_vma=False
    )
```

```python
import functools

import jax
import jax.numpy as jnp
from jax import lax
from jax.experimental import pallas as pl
from jax.experimental.pallas import tpu as pltpu
from jax.sharding import Mesh, PartitionSpec as P

root_two_pi = 0.7978845608028654
cubic = 0.044715

AXES = ("x", "zl", "c", "yh", "yl", "zh")
SIZES = (4, 2, 2, 4, 2, 4)
NX, NZL, NC, _, _, NZH = SIZES
RING = ("yh", "yl")
NY = 8
ROUNDS = NY // 2
LANES = 128
GROUP = 4
NEAR = ("x", "zl", "c", "yl")
FAR = ("yh", "zh")
NEAR_SIZE = 32


def halves(v):
    high = v.astype(jnp.bfloat16)
    return high, (v - high.astype(jnp.float32)).astype(jnp.bfloat16)


def dot3(a, b, dims):
    ah, al = halves(a)
    bh, bl = halves(b)

    def one(u, v):
        return lax.dot_general(u, v, (dims, ((), ())), preferred_element_type=jnp.float32)

    return one(ah, bh) + (one(al, bh) + one(ah, bl))


def gelu_parts(z):
    inner = root_two_pi * (z + cubic * z * z * z)
    slope_t = jnp.tanh(inner)
    value = 0.5 * z * (1.0 + slope_t)
    slope = 0.5 * (1.0 + slope_t) + 0.5 * z * (1.0 - slope_t * slope_t) * root_two_pi * (
        1.0 + 3.0 * cubic * z * z
    )
    return (value, slope)


def trade(v, axis, way):
    n = lax.axis_size(axis)
    return lax.ppermute(v, axis, [(k, (k + 1 - 2 * ((k + way) % 2)) % n) for k in range(n)])


def ahead(place, axis):
    n = lax.axis_size(axis)
    me = lax.axis_index(axis)
    return lax.rem((1 - 2 * (me % 2)) * (place - me) + n, n)


def swap(v, axes):
    return lax.all_to_all(v, axes, split_axis=0, concat_axis=0, tiled=True)


def share(v, axes):
    return swap(jnp.broadcast_to(v[None], (lax.axis_size(axes),) + v.shape), axes)


def slot_plan(tile_rows, tile_cols, tile_count):
    ids = jnp.arange(tile_rows.shape[0], dtype=jnp.int32)
    place = ahead(tile_rows // NZH, RING) * NZH + tile_rows % NZH
    place = jnp.where(ids < tile_count[0], place, NY * NZH)
    core = lax.rem(tile_cols % NC + lax.axis_index("c"), NC)
    return place * 16 + core * (NX * NZL) + tile_cols // NC


def split_kernel(tiles_ref, out_ref):
    for k in range(tiles_ref.shape[0]):
        out_ref[k] = jnp.concatenate(halves(tiles_ref[k]), axis=1)


def split_tiles(tiles):
    slots, tile, _ = tiles.shape
    step = 8
    return pl.pallas_call(
        split_kernel,
        grid=(slots // step,),
        out_shape=jax.ShapeDtypeStruct((slots, tile, 2 * tile), jnp.bfloat16),
        in_specs=[pl.BlockSpec((step, tile, tile), lambda k: (k, 0, 0))],
        out_specs=pl.BlockSpec((step, tile, 2 * tile), lambda k: (k, 0, 0)),
        compiler_params=pltpu.CompilerParams(vmem_limit_bytes=8 * 1024 * 1024),
        cost_estimate=pl.CostEstimate(flops=4 * 10**6, bytes_accessed=8 * 2**20, transcendentals=0),
    )(tiles)


def slot_product(left, high, low):
    tile = left.shape[0]
    return jnp.dot(
        jnp.concatenate([left, left[:, :tile]], axis=1),
        jnp.concatenate([high, high, low], axis=0),
        preferred_element_type=jnp.float32,
    )


def far_kernel(count_ref, plan_ref, left_ref, own_ref, other_ref, out_a_ref, out_b_ref, high, low):
    blocks = own_ref.shape[0]
    for k, source in enumerate((own_ref, other_ref)):
        for b in range(blocks):
            high[k * blocks + b], low[k * blocks + b] = halves(source[b])
    out_a_ref[...] = jnp.zeros_like(out_a_ref)
    out_b_ref[...] = jnp.zeros_like(out_b_ref)

    @pl.loop(0, count_ref[0])
    def _(slot):
        plan = plan_ref[slot]
        place = plan // 16 - ROUNDS * NZH

        @pl.when((place >= 0) & (place < NZH))
        def _():
            value = slot_product(left_ref[slot], high[plan % 16], low[plan % 16])
            out_a_ref[place] += value[:, :LANES]
            out_b_ref[place] += value[:, LANES:]


def far_products(count, plan, left, own, other):
    tile = left.shape[1]
    blocks = jax.ShapeDtypeStruct((2 * own.shape[0], tile, 2 * LANES), jnp.bfloat16)
    smem = pl.BlockSpec(memory_space=pltpu.SMEM)
    vmem = pl.BlockSpec(memory_space=pltpu.VMEM)
    return pl.pallas_call(
        far_kernel,
        out_shape=[jax.ShapeDtypeStruct((NZH, tile, LANES), jnp.float32)] * 2 + [blocks] * 2,
        in_specs=[smem, smem, vmem, vmem, vmem],
        out_specs=[vmem] * 4,
        compiler_params=pltpu.CompilerParams(vmem_limit_bytes=16 * 1024 * 1024),
        cost_estimate=pl.CostEstimate(flops=10**9, bytes_accessed=8 * 2**20, transcendentals=0),
    )(count, plan, left, own, other)


def product_kernel(count_ref, plan_ref, left_ref, high_ref, low_ref, out_a_ref, out_b_ref):
    out_a_ref[...] = jnp.zeros_like(out_a_ref)
    out_b_ref[...] = jnp.zeros_like(out_b_ref)

    @pl.loop(0, (count_ref[0] + GROUP - 1) // GROUP)
    def _(step):
        for k in range(GROUP):
            slot = step * GROUP + k
            plan = plan_ref[slot]
            value = slot_product(left_ref[slot], high_ref[plan % 16], low_ref[plan % 16])
            out_a_ref[plan // 16] += value[:, :LANES]
            out_b_ref[plan // 16] += value[:, LANES:]


def products(count, plan, left, high, low):
    slots, tile, _ = left.shape
    smem = pl.BlockSpec(memory_space=pltpu.SMEM)
    vmem = pl.BlockSpec(memory_space=pltpu.VMEM)
    return pl.pallas_call(
        product_kernel,
        out_shape=[jax.ShapeDtypeStruct((NY * NZH + 1, tile, LANES), jnp.float32)] * 2,
        in_specs=[smem, smem, vmem, vmem, vmem],
        out_specs=[vmem, vmem],
        compiler_params=pltpu.CompilerParams(vmem_limit_bytes=20 * 1024 * 1024),
        cost_estimate=pl.CostEstimate(
            flops=12 * slots * tile * tile * LANES, bytes_accessed=8 * 2**20, transcendentals=0
        ),
    )(count, plan, left, high, low)


def node_kernel(terms_ref, weight_ref, cot_ref, act_ref, grad_ref):
    agg = (terms_ref[0] + terms_ref[1]) + (terms_ref[2] + terms_ref[3])
    pre = dot3(agg, weight_ref[...], ((1,), (0,)))
    value, slope = gelu_parts(pre)
    act_ref[...] = value
    grad = dot3(agg, cot_ref[...] * slope, ((0,), (0,)))
    rows = grad.shape[0] // NEAR_SIZE
    for r in range(NEAR_SIZE):
        for h in range(2):
            grad_ref[r, h] = grad[rows * r : rows * (r + 1), h * LANES : (h + 1) * LANES]


def node_step(terms, weight, cotangent):
    vmem = pl.BlockSpec(memory_space=pltpu.VMEM)
    return pl.pallas_call(
        node_kernel,
        out_shape=(
            jax.ShapeDtypeStruct(cotangent.shape, jnp.float32),
            jax.ShapeDtypeStruct((NEAR_SIZE, 2, weight.shape[0] // NEAR_SIZE, LANES), jnp.float32),
        ),
        in_specs=[vmem] * 3,
        out_specs=(vmem, vmem),
        compiler_params=pltpu.CompilerParams(vmem_limit_bytes=8 * 1024 * 1024),
    )(terms, weight, cotangent)


def after(values, witness):
    here = lax.optimization_barrier((*(v for v in values if v is not None), witness))
    return [None if v is None else here[sum(u is not None for u in values[:k])] for k, v in enumerate(values)]


def chunk(sums, ahead):
    return sums[ahead * NZH : (ahead + 1) * NZH]


def advance(sums, step, got):
    pair = [chunk(sums, ROUNDS - step), chunk(sums, (ROUNDS + step) % NY)]
    if step == ROUNDS:
        return pair[0] + (got[0] + got[1])
    return [v if g is None else v + g for v, g in zip(pair, got[::-1])]


def send(pair):
    return trade(pair[0], RING, 0), trade(pair[1], RING, 1)


def body(features, adjacency_tiles, tile_rows, tile_cols, tile_count, weight, cotangent):
    plan = slot_plan(tile_rows, tile_cols, tile_count)
    own = share(features, ("x", "zl"))
    other = lax.ppermute(own, "c", [(0, 1), (1, 0)])
    left = split_tiles(adjacency_tiles)
    far_a, far_b, high, low = far_products(tile_count, plan, left, own, other)
    got_a = (None, trade(far_a, RING, 1))
    got_b = (trade(far_b, RING, 0), None)
    sums_a, sums_b = products(tile_count, plan, left, high, low)
    out_b = [far_b]
    for step in range(1, ROUNDS):
        out_a = advance(sums_a, step, after(got_a, out_b[0]))
        got_a = send(out_a)
        out_b = advance(sums_b, step, after(got_b, out_a[0]))
        got_b = send(out_b)
    last_a = advance(sums_a, ROUNDS, after(got_a, out_b[0]))
    last_b = advance(sums_b, ROUNDS, after(got_b, last_a))
    terms = swap(jnp.concatenate([last_a, last_b], axis=2), "zh")
    activated, grad = node_step(terms, weight, cotangent)
    grad = jnp.sum(swap(grad, NEAR), axis=0)
    grad = jnp.sum(share(grad, FAR), axis=0)
    grad = share(grad, NEAR)
    width = weight.shape[0]
    weight_grad = grad.swapaxes(1, 2).reshape(width, width)
    return (activated, weight_grad)


def solution(mesh):
    split = Mesh(mesh.devices.reshape(SIZES), AXES)
    placed = (P(AXES, None), P(AXES, None, None), P(AXES), P(AXES), P(AXES), P(), P(AXES, None))
    return jax.shard_map(
        body, mesh=split, in_specs=placed, out_specs=(P(AXES, None), P()), check_vma=False
    )
```

```python
import functools

import jax
import jax.numpy as jnp
from jax import lax
from jax.experimental import pallas as pl
from jax.experimental.pallas import tpu as pltpu
from jax.sharding import Mesh, PartitionSpec as P

root_two_pi = 0.7978845608028654
cubic = 0.044715

AXES = ("x", "zl", "c", "yh", "yl", "zh")
SIZES = (4, 2, 2, 4, 2, 4)
NX, NZL, NC, _, _, NZH = SIZES
RING = ("yh", "yl")
NY = 8
ROUNDS = NY // 2
LANES = 128
GROUP = 4
NEAR = ("x", "zl", "c", "yl")
FAR = ("yh", "zh")
NEAR_SIZE = 32


def halves(v):
    high = v.astype(jnp.bfloat16)
    return high, (v - high.astype(jnp.float32)).astype(jnp.bfloat16)


def dot3(a, b, dims):
    ah, al = halves(a)
    bh, bl = halves(b)

    def one(u, v):
        return lax.dot_general(u, v, (dims, ((), ())), preferred_element_type=jnp.float32)

    return one(ah, bh) + (one(al, bh) + one(ah, bl))


def gelu_parts(z):
    inner = root_two_pi * (z + cubic * z * z * z)
    slope_t = jnp.tanh(inner)
    value = 0.5 * z * (1.0 + slope_t)
    slope = 0.5 * (1.0 + slope_t) + 0.5 * z * (1.0 - slope_t * slope_t) * root_two_pi * (
        1.0 + 3.0 * cubic * z * z
    )
    return (value, slope)


def trade(v, axis, way):
    n = lax.axis_size(axis)
    return lax.ppermute(v, axis, [(k, (k + 1 - 2 * ((k + way) % 2)) % n) for k in range(n)])


def ahead(place, axis):
    n = lax.axis_size(axis)
    me = lax.axis_index(axis)
    return lax.rem((1 - 2 * (me % 2)) * (place - me) + n, n)


def swap(v, axes):
    return lax.all_to_all(v, axes, split_axis=0, concat_axis=0, tiled=True)


def share(v, axes):
    return swap(jnp.broadcast_to(v[None], (lax.axis_size(axes),) + v.shape), axes)


def slot_plan(tile_rows, tile_cols, tile_count):
    ids = jnp.arange(tile_rows.shape[0], dtype=jnp.int32)
    place = ahead(tile_rows // NZH, RING) * NZH + tile_rows % NZH
    place = jnp.where(ids < tile_count[0], place, NY * NZH)
    core = lax.rem(tile_cols % NC + lax.axis_index("c"), NC)
    return place * 16 + core * (NX * NZL) + tile_cols // NC


def split_kernel(tiles_ref, out_ref):
    for k in range(tiles_ref.shape[0]):
        out_ref[k] = jnp.concatenate(halves(tiles_ref[k]), axis=1)


def split_tiles(tiles):
    slots, tile, _ = tiles.shape
    step = 8
    return pl.pallas_call(
        split_kernel,
        grid=(slots // step,),
        out_shape=jax.ShapeDtypeStruct((slots, tile, 2 * tile), jnp.bfloat16),
        in_specs=[pl.BlockSpec((step, tile, tile), lambda k: (k, 0, 0))],
        out_specs=pl.BlockSpec((step, tile, 2 * tile), lambda k: (k, 0, 0)),
        compiler_params=pltpu.CompilerParams(vmem_limit_bytes=8 * 1024 * 1024),
        cost_estimate=pl.CostEstimate(flops=4 * 10**6, bytes_accessed=8 * 2**20, transcendentals=0),
    )(tiles)


def slot_product(left, high, low):
    tile = left.shape[0]
    return jnp.dot(
        jnp.concatenate([left, left[:, :tile]], axis=1),
        jnp.concatenate([high, high, low], axis=0),
        preferred_element_type=jnp.float32,
    )


def far_kernel(count_ref, plan_ref, left_ref, own_ref, other_ref, out_ref, high, low):
    blocks = own_ref.shape[0]
    for k, source in enumerate((own_ref, other_ref)):
        for b in range(blocks):
            high[k * blocks + b], low[k * blocks + b] = halves(source[b])
    out_ref[...] = jnp.zeros_like(out_ref)

    @pl.loop(0, count_ref[0])
    def _(slot):
        plan = plan_ref[slot]
        place = plan // 16 - ROUNDS * NZH

        @pl.when((place >= 0) & (place < NZH))
        def _():
            out_ref[place] += slot_product(left_ref[slot], high[plan % 16], low[plan % 16])


def far_products(count, plan, left, own, other):
    tile = left.shape[1]
    blocks = jax.ShapeDtypeStruct((2 * own.shape[0], tile, 2 * LANES), jnp.bfloat16)
    smem = pl.BlockSpec(memory_space=pltpu.SMEM)
    vmem = pl.BlockSpec(memory_space=pltpu.VMEM)
    return pl.pallas_call(
        far_kernel,
        out_shape=[jax.ShapeDtypeStruct((NZH, tile, 2 * LANES), jnp.float32)] + [blocks] * 2,
        in_specs=[smem, smem, vmem, vmem, vmem],
        out_specs=[vmem] * 3,
        compiler_params=pltpu.CompilerParams(vmem_limit_bytes=16 * 1024 * 1024),
        cost_estimate=pl.CostEstimate(flops=10**9, bytes_accessed=8 * 2**20, transcendentals=0),
    )(count, plan, left, own, other)


def product_kernel(count_ref, plan_ref, left_ref, high_ref, low_ref, out_ref):
    out_ref[...] = jnp.zeros_like(out_ref)

    @pl.loop(0, (count_ref[0] + GROUP - 1) // GROUP)
    def _(step):
        for k in range(GROUP):
            slot = step * GROUP + k
            plan = plan_ref[slot]
            out_ref[plan // 16] += slot_product(
                left_ref[slot], high_ref[plan % 16], low_ref[plan % 16]
            )


def products(count, plan, left, high, low):
    slots, tile, _ = left.shape
    smem = pl.BlockSpec(memory_space=pltpu.SMEM)
    vmem = pl.BlockSpec(memory_space=pltpu.VMEM)
    return pl.pallas_call(
        product_kernel,
        out_shape=jax.ShapeDtypeStruct((NY * NZH + 1, tile, 2 * LANES), jnp.float32),
        in_specs=[smem, smem, vmem, vmem, vmem],
        out_specs=vmem,
        compiler_params=pltpu.CompilerParams(vmem_limit_bytes=20 * 1024 * 1024),
        cost_estimate=pl.CostEstimate(flops=10**6, bytes_accessed=2**16, transcendentals=0),
    )(count, plan, left, high, low)


def node_kernel(terms_ref, weight_ref, cot_ref, act_ref, grad_ref):
    agg = (terms_ref[0] + terms_ref[1]) + (terms_ref[2] + terms_ref[3])
    pre = dot3(agg, weight_ref[...], ((1,), (0,)))
    value, slope = gelu_parts(pre)
    act_ref[...] = value
    grad = dot3(agg, cot_ref[...] * slope, ((0,), (0,)))
    rows = grad.shape[0] // NEAR_SIZE
    for r in range(NEAR_SIZE):
        for h in range(2):
            grad_ref[r, h] = grad[rows * r : rows * (r + 1), h * LANES : (h + 1) * LANES]


def node_step(terms, weight, cotangent):
    vmem = pl.BlockSpec(memory_space=pltpu.VMEM)
    return pl.pallas_call(
        node_kernel,
        out_shape=(
            jax.ShapeDtypeStruct(cotangent.shape, jnp.float32),
            jax.ShapeDtypeStruct((NEAR_SIZE, 2, weight.shape[0] // NEAR_SIZE, LANES), jnp.float32),
        ),
        in_specs=[vmem] * 3,
        out_specs=(vmem, vmem),
        compiler_params=pltpu.CompilerParams(vmem_limit_bytes=8 * 1024 * 1024),
    )(terms, weight, cotangent)


def after(value, witness):
    return lax.optimization_barrier((value, witness))[0]


def chunk(sums, ahead):
    return sums[ahead * NZH : (ahead + 1) * NZH]


def advance(sums, step, way, got):
    part = chunk(sums, (ROUNDS + (2 * way - 1) * step) % NY)
    if step == 1:
        rest = ((0, 0), (0, 0))
        got = jnp.pad(got, ((NZH // 2 * (1 - way), NZH // 2 * way), *rest))
    return part + got


def body(features, adjacency_tiles, tile_rows, tile_cols, tile_count, weight, cotangent):
    plan = slot_plan(tile_rows, tile_cols, tile_count)
    own = share(features, ("x", "zl"))
    other = lax.ppermute(own, "c", [(0, 1), (1, 0)])
    left = split_tiles(adjacency_tiles)
    far, high, low = far_products(tile_count, plan, left, own, other)
    got = [trade(far[: NZH // 2], RING, 0), trade(far[NZH // 2 :], RING, 1)]
    sums = products(tile_count, plan, left, high, low)
    made = sums
    got = lax.optimization_barrier(got)
    first = 1
    for step in range(1, ROUNDS):
        came = got
        got = [None, None]
        for way in (first, 1 - first):
            made = advance(sums, step, way, after(came[1 - way], made))
            got[way] = trade(made, RING, way)
        first = 1 - first
    whole = lax.optimization_barrier(chunk(sums, 0) + after(got[1 - first], made))
    terms = swap(whole + got[first], "zh")
    activated, grad = node_step(terms, weight, cotangent)
    grad = jnp.sum(swap(grad, NEAR), axis=0)
    grad = jnp.sum(share(grad, FAR), axis=0)
    grad = share(grad, NEAR)
    width = weight.shape[0]
    weight_grad = grad.swapaxes(1, 2).reshape(width, width)
    return (activated, weight_grad)


def solution(mesh):
    split = Mesh(mesh.devices.reshape(SIZES), AXES)
    placed = (P(AXES, None), P(AXES, None, None), P(AXES), P(AXES), P(AXES), P(), P(AXES, None))
    return jax.shard_map(
        body, mesh=split, in_specs=placed, out_specs=(P(AXES, None), P()), check_vma=False
    )
```

```python
import functools

import jax
import jax.numpy as jnp
from jax import lax
from jax.experimental import pallas as pl
from jax.experimental.pallas import tpu as pltpu
from jax.sharding import Mesh, PartitionSpec as P

root_two_pi = 0.7978845608028654
cubic = 0.044715

AXES = ("x", "zl", "c", "yh", "yl", "zh")
SIZES = (4, 2, 2, 4, 2, 4)
NX, NZL, NC, _, _, NZH = SIZES
RING = ("yh", "yl")
NY = 8
ROUNDS = NY // 2
LANES = 128
GROUP = 4
NEAR = ("x", "zl", "c", "yl")
FAR = ("yh", "zh")
NEAR_SIZE = 32


def halves(v):
    high = v.astype(jnp.bfloat16)
    return high, (v - high.astype(jnp.float32)).astype(jnp.bfloat16)


def dot3(a, b, dims):
    ah, al = halves(a)
    bh, bl = halves(b)

    def one(u, v):
        return lax.dot_general(u, v, (dims, ((), ())), preferred_element_type=jnp.float32)

    return one(ah, bh) + (one(al, bh) + one(ah, bl))


def gelu_parts(z):
    inner = root_two_pi * (z + cubic * z * z * z)
    slope_t = jnp.tanh(inner)
    value = 0.5 * z * (1.0 + slope_t)
    slope = 0.5 * (1.0 + slope_t) + 0.5 * z * (1.0 - slope_t * slope_t) * root_two_pi * (
        1.0 + 3.0 * cubic * z * z
    )
    return (value, slope)


def trade(v, axis, way):
    n = lax.axis_size(axis)
    return lax.ppermute(v, axis, [(k, (k + 1 - 2 * ((k + way) % 2)) % n) for k in range(n)])


def ahead(place, axis):
    n = lax.axis_size(axis)
    me = lax.axis_index(axis)
    return lax.rem((1 - 2 * (me % 2)) * (place - me) + n, n)


def swap(v, axes):
    return lax.all_to_all(v, axes, split_axis=0, concat_axis=0, tiled=True)


def share(v, axes):
    return swap(jnp.broadcast_to(v[None], (lax.axis_size(axes),) + v.shape), axes)


def slot_plan(tile_rows, tile_cols, tile_count):
    ids = jnp.arange(tile_rows.shape[0], dtype=jnp.int32)
    far = ahead(tile_rows // NZH, RING)
    away = jnp.minimum(far, NY - far)
    key = jnp.where(ids < tile_count[0], jnp.minimum(ROUNDS - away, 2), 3)
    row = tile_rows % NZH + NZH * (
        jnp.where(far > ROUNDS, 1, 0) + jnp.where(away == 1, 3, jnp.where(away == 0, 2, 0))
    )
    core = lax.rem(tile_cols % NC + lax.axis_index("c"), NC)
    packed = (ids * 32 + row) * 16 + core * (NX * NZL) + tile_cols // NC
    before = (key[None, :] < key[:, None]) | (
        (key[None, :] == key[:, None]) & (ids[None, :] < ids[:, None])
    )
    place = jnp.sum(before.astype(jnp.int32), axis=1)
    ordered = jnp.sum(jnp.where(place[None, :] == ids[:, None], packed[None, :], 0), axis=1)
    marks = jnp.arange(8, dtype=jnp.int32)
    starts = jnp.sum((key[None, :] < marks[:, None]).astype(jnp.int32), axis=1)
    return ordered, starts


def split_kernel(tiles_ref, out_ref):
    for k in range(tiles_ref.shape[0]):
        out_ref[k] = jnp.concatenate(halves(tiles_ref[k]), axis=1)


def split_tiles(tiles):
    slots, tile, _ = tiles.shape
    step = 8
    return pl.pallas_call(
        split_kernel,
        grid=(slots // step,),
        out_shape=jax.ShapeDtypeStruct((slots, tile, 2 * tile), jnp.bfloat16),
        in_specs=[pl.BlockSpec((step, tile, tile), lambda k: (k, 0, 0))],
        out_specs=pl.BlockSpec((step, tile, 2 * tile), lambda k: (k, 0, 0)),
        compiler_params=pltpu.CompilerParams(vmem_limit_bytes=8 * 1024 * 1024),
        cost_estimate=pl.CostEstimate(flops=4 * 10**6, bytes_accessed=8 * 2**20, transcendentals=0),
    )(tiles)


def slot_product(left, high, low):
    tile = left.shape[0]
    return jnp.dot(
        jnp.concatenate([left, left[:, :tile]], axis=1),
        jnp.concatenate([high, high, low], axis=0),
        preferred_element_type=jnp.float32,
    )


def add_products(step, starts_ref, order_ref, left_ref, high, low, out_a_ref, out_b_ref):
    first, last = starts_ref[step], starts_ref[step + 1]
    slots, spare = order_ref.shape[0], out_a_ref.shape[0] - 1
    out_a_ref[...] = jnp.zeros_like(out_a_ref)
    out_b_ref[...] = jnp.zeros_like(out_b_ref)

    @pl.loop(0, (last - first + GROUP - 1) // GROUP)
    def _(group):
        for k in range(GROUP):
            index = first + group * GROUP + k
            packed = order_ref[jnp.minimum(index, slots - 1)]
            row = jnp.where(index < last, packed // 16 % 32, spare)
            value = slot_product(left_ref[packed // 512], high[packed % 16], low[packed % 16])
            out_a_ref[row] += value[:, :LANES]
            out_b_ref[row] += value[:, LANES:]


def first_kernel(starts_ref, order_ref, left_ref, own_ref, other_ref, out_a_ref, out_b_ref, high, low):
    blocks = own_ref.shape[0]
    for k, source in enumerate((own_ref, other_ref)):
        for b in range(blocks):
            high[k * blocks + b], low[k * blocks + b] = halves(source[b])
    add_products(0, starts_ref, order_ref, left_ref, high, low, out_a_ref, out_b_ref)


def sums_of(step, starts, ordered, left, sources):
    tile = left.shape[1]
    rows = NZH * (1, 2, 5)[step] + 1
    shapes = [jax.ShapeDtypeStruct((rows, tile, LANES), jnp.float32)] * 2
    if step == 0:
        shapes += [jax.ShapeDtypeStruct((2 * sources[0].shape[0], tile, 2 * LANES), jnp.bfloat16)] * 2
    smem = pl.BlockSpec(memory_space=pltpu.SMEM)
    vmem = pl.BlockSpec(memory_space=pltpu.VMEM)
    return pl.pallas_call(
        functools.partial(add_products, step) if step else first_kernel,
        out_shape=shapes,
        in_specs=[smem, smem, vmem, vmem, vmem],
        out_specs=[vmem] * len(shapes),
        compiler_params=pltpu.CompilerParams(vmem_limit_bytes=16 * 1024 * 1024),
        cost_estimate=pl.CostEstimate(flops=10**6, bytes_accessed=2**14, transcendentals=0),
    )(starts, ordered, left, *sources)


def node_kernel(terms_ref, weight_ref, cot_ref, act_ref, grad_ref):
    agg = (terms_ref[0] + terms_ref[1]) + (terms_ref[2] + terms_ref[3])
    pre = dot3(agg, weight_ref[...], ((1,), (0,)))
    value, slope = gelu_parts(pre)
    act_ref[...] = value
    grad = dot3(agg, cot_ref[...] * slope, ((0,), (0,)))
    rows = grad.shape[0] // NEAR_SIZE
    for r in range(NEAR_SIZE):
        for h in range(2):
            grad_ref[r, h] = grad[rows * r : rows * (r + 1), h * LANES : (h + 1) * LANES]


def node_step(terms, weight, cotangent):
    vmem = pl.BlockSpec(memory_space=pltpu.VMEM)
    return pl.pallas_call(
        node_kernel,
        out_shape=(
            jax.ShapeDtypeStruct(cotangent.shape, jnp.float32),
            jax.ShapeDtypeStruct((NEAR_SIZE, 2, weight.shape[0] // NEAR_SIZE, LANES), jnp.float32),
        ),
        in_specs=[vmem] * 3,
        out_specs=(vmem, vmem),
        compiler_params=pltpu.CompilerParams(vmem_limit_bytes=8 * 1024 * 1024),
    )(terms, weight, cotangent)


def after(values, witness):
    here = lax.optimization_barrier((*(v for v in values if v is not None), witness))
    return [None if v is None else here[sum(u is not None for u in values[:k])] for k, v in enumerate(values)]


def advance(sums, first, got):
    pair = [sums[first : first + NZH], sums[first + NZH : first + 2 * NZH]]
    return [v if g is None else v + g for v, g in zip(pair, got[::-1])]


def finish(sums, got):
    return sums[2 * NZH : 3 * NZH] + (got[0] + got[1])


def send(pair):
    return trade(pair[0], RING, 0), trade(pair[1], RING, 1)


def body(features, adjacency_tiles, tile_rows, tile_cols, tile_count, weight, cotangent):
    ordered, starts = slot_plan(tile_rows, tile_cols, tile_count)
    own = share(features, ("x", "zl"))
    other = lax.ppermute(own, "c", [(0, 1), (1, 0)])
    left = split_tiles(adjacency_tiles)
    far_a, far_b, high, low = sums_of(0, starts, ordered, left, (own, other))
    far_a, far_b = far_a[:NZH], far_b[:NZH]
    got_a = (None, trade(far_a, RING, 1))
    got_b = (trade(far_b, RING, 0), None)
    out_b = [far_b]
    for step in range(1, ROUNDS):
        if step < 3:
            sums_a, sums_b = sums_of(step, after((starts,), out_b[0])[0], ordered, left, (high, low))
        first = 0 if step < 3 else 3 * NZH
        out_a = advance(sums_a, first, after(got_a, out_b[0]))
        got_a = send(out_a)
        out_b = advance(sums_b, first, after(got_b, out_a[0]))
        got_b = send(out_b)
    last_a = finish(sums_a, after(got_a, out_b[0]))
    last_b = finish(sums_b, after(got_b, last_a))
    terms = swap(jnp.concatenate([last_a, last_b], axis=2), "zh")
    activated, grad = node_step(terms, weight, cotangent)
    grad = jnp.sum(swap(grad, NEAR), axis=0)
    grad = jnp.sum(share(grad, FAR), axis=0)
    grad = share(grad, NEAR)
    width = weight.shape[0]
    weight_grad = grad.swapaxes(1, 2).reshape(width, width)
    return (activated, weight_grad)


def solution(mesh):
    split = Mesh(mesh.devices.reshape(SIZES), AXES)
    placed = (P(AXES, None), P(AXES, None, None), P(AXES), P(AXES), P(AXES), P(), P(AXES, None))
    return jax.shard_map(
        body, mesh=split, in_specs=placed, out_specs=(P(AXES, None), P()), check_vma=False
    )
```

```python
import functools

import jax
import jax.numpy as jnp
from jax import lax
from jax.experimental import pallas as pl
from jax.experimental.pallas import tpu as pltpu
from jax.sharding import Mesh, PartitionSpec as P

root_two_pi = 0.7978845608028654
cubic = 0.044715

AXES = ("x", "zl", "c", "yh", "yl", "zh")
SIZES = (4, 2, 2, 4, 2, 4)
NX, NZL, NC, _, _, NZH = SIZES
RING = ("yh", "yl")
NY = 8
ROUNDS = NY // 2
LANES = 128
GROUP = 4
NEAR = ("x", "zl", "c", "yl")
FAR = ("yh", "zh")
NEAR_SIZE = 32
PARTS = (10, 11, 8, 2, 1, 0, 9, 12)
MESSAGES = (
    (0, 0, 3), (1, 1, 5), (0, 0, 2), (1, 1, 6), (0, 1, 6),
    (1, 0, 2), (0, 1, 7), (1, 0, 1), (0, 0, 1), (1, 1, 7),
)


def halves(v):
    high = v.astype(jnp.bfloat16)
    return high, (v - high.astype(jnp.float32)).astype(jnp.bfloat16)


def dot3(a, b, dims):
    ah, al = halves(a)
    bh, bl = halves(b)

    def one(u, v):
        return lax.dot_general(u, v, (dims, ((), ())), preferred_element_type=jnp.float32)

    return one(ah, bh) + (one(al, bh) + one(ah, bl))


def gelu_parts(z):
    inner = root_two_pi * (z + cubic * z * z * z)
    slope_t = jnp.tanh(inner)
    value = 0.5 * z * (1.0 + slope_t)
    slope = 0.5 * (1.0 + slope_t) + 0.5 * z * (1.0 - slope_t * slope_t) * root_two_pi * (
        1.0 + 3.0 * cubic * z * z
    )
    return (value, slope)


def trade(v, axis, way):
    n = lax.axis_size(axis)
    return lax.ppermute(v, axis, [(k, (k + 1 - 2 * ((k + way) % 2)) % n) for k in range(n)])


def ahead(place, axis):
    n = lax.axis_size(axis)
    me = lax.axis_index(axis)
    return lax.rem((1 - 2 * (me % 2)) * (place - me) + n, n)


def swap(v, axes):
    return lax.all_to_all(v, axes, split_axis=0, concat_axis=0, tiled=True)


def share(v, axes):
    return swap(jnp.broadcast_to(v[None], (lax.axis_size(axes),) + v.shape), axes)


def slot_plan(tile_rows, tile_cols, tile_count):
    ids = jnp.arange(tile_rows.shape[0], dtype=jnp.int32)
    far = ahead(tile_rows // NZH, RING)
    part = sum(jnp.where(far == k, PARTS[k], 0) for k in range(NY))
    key = jnp.where(ids < tile_count[0], part // 8, 2)
    row = tile_rows % NZH + part % 8 * NZH
    core = lax.rem(tile_cols % NC + lax.axis_index("c"), NC)
    packed = (ids * 32 + row) * 16 + core * (NX * NZL) + tile_cols // NC
    before = (key[None, :] < key[:, None]) | (
        (key[None, :] == key[:, None]) & (ids[None, :] < ids[:, None])
    )
    place = jnp.sum(before.astype(jnp.int32), axis=1)
    ordered = jnp.sum(jnp.where(place[None, :] == ids[:, None], packed[None, :], 0), axis=1)
    marks = jnp.arange(8, dtype=jnp.int32)
    starts = jnp.sum((key[None, :] < marks[:, None]).astype(jnp.int32), axis=1)
    return ordered, starts


def split_kernel(tiles_ref, out_ref):
    for k in range(tiles_ref.shape[0]):
        out_ref[k] = jnp.concatenate(halves(tiles_ref[k]), axis=1)


def split_tiles(tiles):
    slots, tile, _ = tiles.shape
    step = 8
    return pl.pallas_call(
        split_kernel,
        grid=(slots // step,),
        out_shape=jax.ShapeDtypeStruct((slots, tile, 2 * tile), jnp.bfloat16),
        in_specs=[pl.BlockSpec((step, tile, tile), lambda k: (k, 0, 0))],
        out_specs=pl.BlockSpec((step, tile, 2 * tile), lambda k: (k, 0, 0)),
        compiler_params=pltpu.CompilerParams(vmem_limit_bytes=8 * 1024 * 1024),
        cost_estimate=pl.CostEstimate(flops=4 * 10**6, bytes_accessed=8 * 2**20, transcendentals=0),
    )(tiles)


def slot_product(left, high, low):
    tile = left.shape[0]
    return jnp.dot(
        jnp.concatenate([left, left[:, :tile]], axis=1),
        jnp.concatenate([high, high, low], axis=0),
        preferred_element_type=jnp.float32,
    )


def add_products(step, starts_ref, order_ref, left_ref, high, low, out_a_ref, out_b_ref):
    first, last = starts_ref[step], starts_ref[step + 1]
    slots, spare = order_ref.shape[0], out_a_ref.shape[0] - 1
    out_a_ref[...] = jnp.zeros_like(out_a_ref)
    out_b_ref[...] = jnp.zeros_like(out_b_ref)

    @pl.loop(0, (last - first + GROUP - 1) // GROUP)
    def _(group):
        for k in range(GROUP):
            index = first + group * GROUP + k
            packed = order_ref[jnp.minimum(index, slots - 1)]
            row = jnp.where(index < last, packed // 16 % 32, spare)
            value = slot_product(left_ref[packed // 512], high[packed % 16], low[packed % 16])
            out_a_ref[row] += value[:, :LANES]
            out_b_ref[row] += value[:, LANES:]


def first_kernel(starts_ref, order_ref, left_ref, own_ref, other_ref, out_a_ref, out_b_ref, high, low):
    blocks = own_ref.shape[0]
    for k, source in enumerate((own_ref, other_ref)):
        for b in range(blocks):
            high[k * blocks + b], low[k * blocks + b] = halves(source[b])
    add_products(0, starts_ref, order_ref, left_ref, high, low, out_a_ref, out_b_ref)


def sums_of(step, starts, ordered, left, sources):
    tile = left.shape[1]
    rows = NZH * (3, 5)[step] + 1
    shapes = [jax.ShapeDtypeStruct((rows, tile, LANES), jnp.float32)] * 2
    if step == 0:
        shapes += [jax.ShapeDtypeStruct((2 * sources[0].shape[0], tile, 2 * LANES), jnp.bfloat16)] * 2
    smem = pl.BlockSpec(memory_space=pltpu.SMEM)
    vmem = pl.BlockSpec(memory_space=pltpu.VMEM)
    return pl.pallas_call(
        functools.partial(add_products, step) if step else first_kernel,
        out_shape=shapes,
        in_specs=[smem, smem, vmem, vmem, vmem],
        out_specs=[vmem] * len(shapes),
        compiler_params=pltpu.CompilerParams(vmem_limit_bytes=16 * 1024 * 1024),
        cost_estimate=pl.CostEstimate(flops=10**6, bytes_accessed=2**14, transcendentals=0),
    )(starts, ordered, left, *sources)


def node_kernel(terms_ref, weight_ref, cot_ref, act_ref, grad_ref):
    agg = (terms_ref[0] + terms_ref[1]) + (terms_ref[2] + terms_ref[3])
    pre = dot3(agg, weight_ref[...], ((1,), (0,)))
    value, slope = gelu_parts(pre)
    act_ref[...] = value
    grad = dot3(agg, cot_ref[...] * slope, ((0,), (0,)))
    rows = grad.shape[0] // NEAR_SIZE
    for r in range(NEAR_SIZE):
        for h in range(2):
            grad_ref[r, h] = grad[rows * r : rows * (r + 1), h * LANES : (h + 1) * LANES]


def node_step(terms, weight, cotangent):
    vmem = pl.BlockSpec(memory_space=pltpu.VMEM)
    return pl.pallas_call(
        node_kernel,
        out_shape=(
            jax.ShapeDtypeStruct(cotangent.shape, jnp.float32),
            jax.ShapeDtypeStruct((NEAR_SIZE, 2, weight.shape[0] // NEAR_SIZE, LANES), jnp.float32),
        ),
        in_specs=[vmem] * 3,
        out_specs=(vmem, vmem),
        compiler_params=pltpu.CompilerParams(vmem_limit_bytes=8 * 1024 * 1024),
    )(terms, weight, cotangent)


def after(value, witness):
    return lax.optimization_barrier((value, witness))[0]


def body(features, adjacency_tiles, tile_rows, tile_cols, tile_count, weight, cotangent):
    ordered, starts = slot_plan(tile_rows, tile_cols, tile_count)
    own = share(features, ("x", "zl"))
    other = lax.ppermute(own, "c", [(0, 1), (1, 0)])
    left = split_tiles(adjacency_tiles)
    *early, high, low = sums_of(0, starts, ordered, left, (own, other))
    late = sums_of(1, after(starts, early[0]), ordered, left, (high, low))

    def chunk(lane, far):
        first = PARTS[far] % 8 * NZH
        return (early, late)[PARTS[far] // 8][lane][first : first + NZH]

    first_a = trade(early[0][: 2 * NZH], RING, 1)
    first_b = trade(early[1][NZH : 3 * NZH], RING, 0)
    came = [first_a[NZH:], first_b[:NZH], first_a[:NZH], first_b[NZH:]]
    made = late[0]
    for k, (lane, way, far) in enumerate(MESSAGES):
        made = chunk(lane, far) + after(came[k], made)
        came.append(trade(made, RING, way))
    part_a = chunk(0, 0) + after(came[10], made)
    part_b = chunk(1, 0) + after(came[11], part_a)
    last_a = part_a + after(came[12], part_b)
    last_b = part_b + after(came[13], last_a)
    terms = swap(jnp.concatenate([last_a, last_b], axis=2), "zh")
    activated, grad = node_step(terms, weight, cotangent)
    grad = jnp.sum(swap(grad, NEAR), axis=0)
    grad = jnp.sum(share(grad, FAR), axis=0)
    grad = share(grad, NEAR)
    width = weight.shape[0]
    weight_grad = grad.swapaxes(1, 2).reshape(width, width)
    return (activated, weight_grad)


def solution(mesh):
    split = Mesh(mesh.devices.reshape(SIZES), AXES)
    placed = (P(AXES, None), P(AXES, None, None), P(AXES), P(AXES), P(AXES), P(), P(AXES, None))
    return jax.shard_map(
        body, mesh=split, in_specs=placed, out_specs=(P(AXES, None), P()), check_vma=False
    )
```

```python
import functools

import jax
import jax.numpy as jnp
from jax import lax
from jax.experimental import pallas as pl
from jax.experimental.pallas import tpu as pltpu
from jax.sharding import Mesh, PartitionSpec as P

root_two_pi = 0.7978845608028654
cubic = 0.044715

AXES = ("x", "zl", "c", "yh", "yl", "zh")
SIZES = (4, 2, 2, 4, 2, 4)
NX, NZL, NC, _, _, NZH = SIZES
RING = ("yh", "yl")
NY = 8
ROUNDS = NY // 2
LANES = 128
GROUP = 4
NEAR = ("x", "zl", "c", "yl")
FAR = ("yh", "zh")
NEAR_SIZE = 32
PARTS = (10, 11, 8, 2, 1, 0, 9, 12)
MESSAGES = (
    (0, 0, 3), (1, 1, 5), (0, 0, 2), (1, 1, 6), (0, 1, 6),
    (1, 0, 2), (0, 1, 7), (1, 0, 1), (0, 0, 1), (1, 1, 7),
)


def halves(v):
    high = v.astype(jnp.bfloat16)
    return high, (v - high.astype(jnp.float32)).astype(jnp.bfloat16)


def dot3(a, b, dims):
    ah, al = halves(a)
    bh, bl = halves(b)

    def one(u, v):
        return lax.dot_general(u, v, (dims, ((), ())), preferred_element_type=jnp.float32)

    return one(ah, bh) + (one(al, bh) + one(ah, bl))


def gelu_parts(z):
    inner = root_two_pi * (z + cubic * z * z * z)
    slope_t = jnp.tanh(inner)
    value = 0.5 * z * (1.0 + slope_t)
    slope = 0.5 * (1.0 + slope_t) + 0.5 * z * (1.0 - slope_t * slope_t) * root_two_pi * (
        1.0 + 3.0 * cubic * z * z
    )
    return (value, slope)


def trade(v, axis, way):
    n = lax.axis_size(axis)
    return lax.ppermute(v, axis, [(k, (k + 1 - 2 * ((k + way) % 2)) % n) for k in range(n)])


def ahead(place, axis):
    n = lax.axis_size(axis)
    me = lax.axis_index(axis)
    return lax.rem((1 - 2 * (me % 2)) * (place - me) + n, n)


def swap(v, axes):
    return lax.all_to_all(v, axes, split_axis=0, concat_axis=0, tiled=True)


def share(v, axes):
    return swap(jnp.broadcast_to(v[None], (lax.axis_size(axes),) + v.shape), axes)


def slot_plan(tile_rows, tile_cols, tile_count):
    ids = jnp.arange(tile_rows.shape[0], dtype=jnp.int32)
    far = ahead(tile_rows // NZH, RING)
    part = sum(jnp.where(far == k, PARTS[k], 0) for k in range(NY))
    key = jnp.where(ids < tile_count[0], part // 8, 2)
    row = tile_rows % NZH + part % 8 * NZH
    core = lax.rem(tile_cols % NC + lax.axis_index("c"), NC)
    packed = (ids * 32 + row) * 16 + core * (NX * NZL) + tile_cols // NC
    before = (key[None, :] < key[:, None]) | (
        (key[None, :] == key[:, None]) & (ids[None, :] < ids[:, None])
    )
    place = jnp.sum(before.astype(jnp.int32), axis=1)
    ordered = jnp.sum(jnp.where(place[None, :] == ids[:, None], packed[None, :], 0), axis=1)
    marks = jnp.arange(8, dtype=jnp.int32)
    starts = jnp.sum((key[None, :] < marks[:, None]).astype(jnp.int32), axis=1)
    return ordered, starts


def split_kernel(tiles_ref, out_ref):
    for k in range(tiles_ref.shape[0]):
        out_ref[k] = jnp.concatenate(halves(tiles_ref[k]), axis=1)


def split_tiles(tiles):
    slots, tile, _ = tiles.shape
    step = 8
    return pl.pallas_call(
        split_kernel,
        grid=(slots // step,),
        out_shape=jax.ShapeDtypeStruct((slots, tile, 2 * tile), jnp.bfloat16),
        in_specs=[pl.BlockSpec((step, tile, tile), lambda k: (k, 0, 0))],
        out_specs=pl.BlockSpec((step, tile, 2 * tile), lambda k: (k, 0, 0)),
        compiler_params=pltpu.CompilerParams(vmem_limit_bytes=8 * 1024 * 1024),
        cost_estimate=pl.CostEstimate(flops=4 * 10**6, bytes_accessed=8 * 2**20, transcendentals=0),
    )(tiles)


def slot_product(left, high, low):
    tile = left.shape[0]
    return jnp.dot(
        jnp.concatenate([left, left[:, :tile]], axis=1),
        jnp.concatenate([high, high, low], axis=0),
        preferred_element_type=jnp.float32,
    )


def add_products(step, starts_ref, order_ref, left_ref, high, low, out_a_ref, out_b_ref):
    first, last = starts_ref[step], starts_ref[step + 1]
    slots, spare = order_ref.shape[0], out_a_ref.shape[0] - 1
    out_a_ref[...] = jnp.zeros_like(out_a_ref)
    out_b_ref[...] = jnp.zeros_like(out_b_ref)

    @pl.loop(0, (last - first + GROUP - 1) // GROUP)
    def _(group):
        for k in range(GROUP):
            index = first + group * GROUP + k
            packed = order_ref[jnp.minimum(index, slots - 1)]
            row = jnp.where(index < last, packed // 16 % 32, spare)
            value = slot_product(left_ref[packed // 512], high[packed % 16], low[packed % 16])
            out_a_ref[row] += value[:, :LANES]
            out_b_ref[row] += value[:, LANES:]


def first_kernel(starts_ref, order_ref, left_ref, own_ref, other_ref, out_a_ref, out_b_ref, high, low):
    blocks = own_ref.shape[0]
    for k, source in enumerate((own_ref, other_ref)):
        for b in range(blocks):
            high[k * blocks + b], low[k * blocks + b] = halves(source[b])
    add_products(0, starts_ref, order_ref, left_ref, high, low, out_a_ref, out_b_ref)


def sums_of(step, starts, ordered, left, sources):
    tile = left.shape[1]
    rows = NZH * (3, 5)[step] + 1
    shapes = [jax.ShapeDtypeStruct((rows, tile, LANES), jnp.float32)] * 2
    if step == 0:
        shapes += [jax.ShapeDtypeStruct((2 * sources[0].shape[0], tile, 2 * LANES), jnp.bfloat16)] * 2
    smem = pl.BlockSpec(memory_space=pltpu.SMEM)
    vmem = pl.BlockSpec(memory_space=pltpu.VMEM)
    return pl.pallas_call(
        functools.partial(add_products, step) if step else first_kernel,
        out_shape=shapes,
        in_specs=[smem, smem, vmem, vmem, vmem],
        out_specs=[vmem] * len(shapes),
        compiler_params=pltpu.CompilerParams(vmem_limit_bytes=16 * 1024 * 1024),
        cost_estimate=pl.CostEstimate(flops=10**6, bytes_accessed=2**14, transcendentals=0),
    )(starts, ordered, left, *sources)


def node_kernel(terms_ref, weight_ref, cot_ref, act_ref, grad_ref):
    agg = (terms_ref[0] + terms_ref[1]) + (terms_ref[2] + terms_ref[3])
    pre = dot3(agg, weight_ref[...], ((1,), (0,)))
    value, slope = gelu_parts(pre)
    act_ref[...] = value
    grad = dot3(agg, cot_ref[...] * slope, ((0,), (0,)))
    rows = grad.shape[0] // NEAR_SIZE
    for r in range(NEAR_SIZE):
        for h in range(2):
            grad_ref[r, h] = grad[rows * r : rows * (r + 1), h * LANES : (h + 1) * LANES]


def node_step(terms, weight, cotangent):
    vmem = pl.BlockSpec(memory_space=pltpu.VMEM)
    return pl.pallas_call(
        node_kernel,
        out_shape=(
            jax.ShapeDtypeStruct(cotangent.shape, jnp.float32),
            jax.ShapeDtypeStruct((NEAR_SIZE, 2, weight.shape[0] // NEAR_SIZE, LANES), jnp.float32),
        ),
        in_specs=[vmem] * 3,
        out_specs=(vmem, vmem),
        compiler_params=pltpu.CompilerParams(vmem_limit_bytes=8 * 1024 * 1024),
    )(terms, weight, cotangent)


def after(value, witness):
    return lax.optimization_barrier((value, witness))[0]


def body(features, adjacency_tiles, tile_rows, tile_cols, tile_count, weight, cotangent):
    ordered, starts = slot_plan(tile_rows, tile_cols, tile_count)
    own = share(features, ("x", "zl"))
    other = lax.ppermute(own, "c", [(0, 1), (1, 0)])
    left = split_tiles(adjacency_tiles)
    *early, high, low = sums_of(0, starts, ordered, left, (own, other))
    late = sums_of(1, after(starts, early[0]), ordered, left, (high, low))

    def chunk(lane, far):
        first = PARTS[far] % 8 * NZH
        return (early, late)[PARTS[far] // 8][lane][first : first + NZH]

    far_a = trade(chunk(0, 4), RING, 1)
    first_b = trade(early[1][NZH : 3 * NZH], RING, 0)
    came = [far_a, first_b[:NZH], trade(chunk(0, 5), RING, 1), first_b[NZH:]]
    made = late[0]
    for k, (lane, way, far) in enumerate(MESSAGES):
        made = chunk(lane, far) + after(came[k], made)
        came.append(trade(made, RING, way))
    part_a = chunk(0, 0) + after(came[10], made)
    part_b = chunk(1, 0) + after(came[11], part_a)
    last_a = part_a + after(came[12], part_b)
    last_b = part_b + after(came[13], last_a)
    terms = swap(jnp.concatenate([last_a, last_b], axis=2), "zh")
    activated, grad = node_step(terms, weight, cotangent)
    grad = jnp.sum(swap(grad, NEAR), axis=0)
    grad = jnp.sum(share(grad, FAR), axis=0)
    grad = share(grad, NEAR)
    width = weight.shape[0]
    weight_grad = grad.swapaxes(1, 2).reshape(width, width)
    return (activated, weight_grad)


def solution(mesh):
    split = Mesh(mesh.devices.reshape(SIZES), AXES)
    placed = (P(AXES, None), P(AXES, None, None), P(AXES), P(AXES), P(AXES), P(), P(AXES, None))
    return jax.shard_map(
        body, mesh=split, in_specs=placed, out_specs=(P(AXES, None), P()), check_vma=False
    )
```

```python
import functools

import jax
import jax.numpy as jnp
from jax import lax
from jax.experimental import pallas as pl
from jax.experimental.pallas import tpu as pltpu
from jax.sharding import Mesh, PartitionSpec as P

root_two_pi = 0.7978845608028654
cubic = 0.044715

AXES = ("x", "zl", "c", "yh", "yl", "zh")
SIZES = (4, 2, 2, 4, 2, 4)
NX, NZL, NC, _, _, NZH = SIZES
RING = ("yh", "yl")
NY = 8
ROUNDS = NY // 2
LANES = 128
GROUP = 4
NEAR = ("x", "zl", "c", "yl")
FAR = ("yh", "zh")
NEAR_SIZE = 32
PARTS = (10, 11, 8, 2, 1, 0, 9, 12)
MESSAGES = (
    (0, 0, 3), (1, 1, 5), (0, 0, 2), (1, 1, 6), (0, 1, 6),
    (1, 0, 2), (0, 1, 7), (1, 0, 1), (0, 0, 1), (1, 1, 7),
)


def halves(v):
    high = v.astype(jnp.bfloat16)
    return high, (v - high.astype(jnp.float32)).astype(jnp.bfloat16)


def dot3(a, b, dims):
    ah, al = halves(a)
    bh, bl = halves(b)

    def one(u, v):
        return lax.dot_general(u, v, (dims, ((), ())), preferred_element_type=jnp.float32)

    return one(ah, bh) + (one(al, bh) + one(ah, bl))


def gelu_parts(z):
    inner = root_two_pi * (z + cubic * z * z * z)
    slope_t = jnp.tanh(inner)
    value = 0.5 * z * (1.0 + slope_t)
    slope = 0.5 * (1.0 + slope_t) + 0.5 * z * (1.0 - slope_t * slope_t) * root_two_pi * (
        1.0 + 3.0 * cubic * z * z
    )
    return (value, slope)


def trade(v, axis, way):
    n = lax.axis_size(axis)
    pairs = [
        (c * n + k, c * n + (k + 1 - 2 * ((k + way + c) % 2)) % n) for c in range(NC) for k in range(n)
    ]
    return lax.ppermute(v, ("c", *axis), pairs)


def ahead(place, axis):
    n = lax.axis_size(axis)
    me = lax.axis_index(axis)
    turn = (me + lax.axis_index("c")) % 2
    return lax.rem((1 - 2 * turn) * (place - me) + n, n)


def swap(v, axes):
    return lax.all_to_all(v, axes, split_axis=0, concat_axis=0, tiled=True)


def share(v, axes):
    return swap(jnp.broadcast_to(v[None], (lax.axis_size(axes),) + v.shape), axes)


def slot_plan(tile_rows, tile_cols, tile_count):
    ids = jnp.arange(tile_rows.shape[0], dtype=jnp.int32)
    far = ahead(tile_rows // NZH, RING)
    part = sum(jnp.where(far == k, PARTS[k], 0) for k in range(NY))
    key = jnp.where(ids < tile_count[0], part // 8, 2)
    row = tile_rows % NZH + part % 8 * NZH
    core = lax.rem(tile_cols % NC + lax.axis_index("c"), NC)
    packed = (ids * 32 + row) * 16 + core * (NX * NZL) + tile_cols // NC
    before = (key[None, :] < key[:, None]) | (
        (key[None, :] == key[:, None]) & (ids[None, :] < ids[:, None])
    )
    place = jnp.sum(before.astype(jnp.int32), axis=1)
    ordered = jnp.sum(jnp.where(place[None, :] == ids[:, None], packed[None, :], 0), axis=1)
    marks = jnp.arange(8, dtype=jnp.int32)
    starts = jnp.sum((key[None, :] < marks[:, None]).astype(jnp.int32), axis=1)
    return ordered, starts


def split_kernel(tiles_ref, out_ref):
    for k in range(tiles_ref.shape[0]):
        out_ref[k] = jnp.concatenate(halves(tiles_ref[k]), axis=1)


def split_tiles(tiles):
    slots, tile, _ = tiles.shape
    step = 8
    return pl.pallas_call(
        split_kernel,
        grid=(slots // step,),
        out_shape=jax.ShapeDtypeStruct((slots, tile, 2 * tile), jnp.bfloat16),
        in_specs=[pl.BlockSpec((step, tile, tile), lambda k: (k, 0, 0))],
        out_specs=pl.BlockSpec((step, tile, 2 * tile), lambda k: (k, 0, 0)),
        compiler_params=pltpu.CompilerParams(vmem_limit_bytes=8 * 1024 * 1024),
        cost_estimate=pl.CostEstimate(flops=4 * 10**6, bytes_accessed=8 * 2**20, transcendentals=0),
    )(tiles)


def slot_product(left, high, low):
    tile = left.shape[0]
    return jnp.dot(
        jnp.concatenate([left, left[:, :tile]], axis=1),
        jnp.concatenate([high, high, low], axis=0),
        preferred_element_type=jnp.float32,
    )


def add_products(step, starts_ref, order_ref, left_ref, high, low, out_a_ref, out_b_ref):
    first, last = starts_ref[step], starts_ref[step + 1]
    slots, spare = order_ref.shape[0], out_a_ref.shape[0] - 1
    out_a_ref[...] = jnp.zeros_like(out_a_ref)
    out_b_ref[...] = jnp.zeros_like(out_b_ref)

    @pl.loop(0, (last - first + GROUP - 1) // GROUP)
    def _(group):
        for k in range(GROUP):
            index = first + group * GROUP + k
            packed = order_ref[jnp.minimum(index, slots - 1)]
            row = jnp.where(index < last, packed // 16 % 32, spare)
            value = slot_product(left_ref[packed // 512], high[packed % 16], low[packed % 16])
            out_a_ref[row] += value[:, :LANES]
            out_b_ref[row] += value[:, LANES:]


def first_kernel(starts_ref, order_ref, left_ref, own_ref, other_ref, out_a_ref, out_b_ref, high, low):
    blocks = own_ref.shape[0]
    for k, source in enumerate((own_ref, other_ref)):
        for b in range(blocks):
            high[k * blocks + b], low[k * blocks + b] = halves(source[b])
    add_products(0, starts_ref, order_ref, left_ref, high, low, out_a_ref, out_b_ref)


def sums_of(step, starts, ordered, left, sources):
    tile = left.shape[1]
    rows = NZH * (3, 5)[step] + 1
    shapes = [jax.ShapeDtypeStruct((rows, tile, LANES), jnp.float32)] * 2
    if step == 0:
        shapes += [jax.ShapeDtypeStruct((2 * sources[0].shape[0], tile, 2 * LANES), jnp.bfloat16)] * 2
    smem = pl.BlockSpec(memory_space=pltpu.SMEM)
    vmem = pl.BlockSpec(memory_space=pltpu.VMEM)
    return pl.pallas_call(
        functools.partial(add_products, step) if step else first_kernel,
        out_shape=shapes,
        in_specs=[smem, smem, vmem, vmem, vmem],
        out_specs=[vmem] * len(shapes),
        compiler_params=pltpu.CompilerParams(vmem_limit_bytes=16 * 1024 * 1024),
        cost_estimate=pl.CostEstimate(flops=10**6, bytes_accessed=2**14, transcendentals=0),
    )(starts, ordered, left, *sources)


def node_kernel(terms_ref, weight_ref, cot_ref, act_ref, grad_ref):
    agg = (terms_ref[0] + terms_ref[1]) + (terms_ref[2] + terms_ref[3])
    pre = dot3(agg, weight_ref[...], ((1,), (0,)))
    value, slope = gelu_parts(pre)
    act_ref[...] = value
    grad = dot3(agg, cot_ref[...] * slope, ((0,), (0,)))
    rows = grad.shape[0] // NEAR_SIZE
    for r in range(NEAR_SIZE):
        for h in range(2):
            grad_ref[r, h] = grad[rows * r : rows * (r + 1), h * LANES : (h + 1) * LANES]


def node_step(terms, weight, cotangent):
    vmem = pl.BlockSpec(memory_space=pltpu.VMEM)
    return pl.pallas_call(
        node_kernel,
        out_shape=(
            jax.ShapeDtypeStruct(cotangent.shape, jnp.float32),
            jax.ShapeDtypeStruct((NEAR_SIZE, 2, weight.shape[0] // NEAR_SIZE, LANES), jnp.float32),
        ),
        in_specs=[vmem] * 3,
        out_specs=(vmem, vmem),
        compiler_params=pltpu.CompilerParams(vmem_limit_bytes=8 * 1024 * 1024),
    )(terms, weight, cotangent)


def after(value, witness):
    return lax.optimization_barrier((value, witness))[0]


def body(features, adjacency_tiles, tile_rows, tile_cols, tile_count, weight, cotangent):
    ordered, starts = slot_plan(tile_rows, tile_cols, tile_count)
    own = share(features, ("x", "zl"))
    other = lax.ppermute(own, "c", [(0, 1), (1, 0)])
    left = split_tiles(adjacency_tiles)
    *early, high, low = sums_of(0, starts, ordered, left, (own, other))
    late = sums_of(1, after(starts, early[0]), ordered, left, (high, low))

    def chunk(lane, far):
        first = PARTS[far] % 8 * NZH
        return (early, late)[PARTS[far] // 8][lane][first : first + NZH]

    first_a = trade(early[0][: 2 * NZH], RING, 1)
    first_b = trade(early[1][NZH : 3 * NZH], RING, 0)
    came = [first_a[NZH:], first_b[:NZH], first_a[:NZH], first_b[NZH:]]
    made = late[0]
    for k, (lane, way, far) in enumerate(MESSAGES):
        made = chunk(lane, far) + after(came[k], made)
        came.append(trade(made, RING, way))
    part_a = chunk(0, 0) + after(came[10], made)
    part_b = chunk(1, 0) + after(came[11], part_a)
    last_a = part_a + after(came[12], part_b)
    last_b = part_b + after(came[13], last_a)
    terms = swap(jnp.concatenate([last_a, last_b], axis=2), "zh")
    activated, grad = node_step(terms, weight, cotangent)
    grad = jnp.sum(swap(grad, NEAR), axis=0)
    grad = jnp.sum(share(grad, FAR), axis=0)
    grad = share(grad, NEAR)
    width = weight.shape[0]
    weight_grad = grad.swapaxes(1, 2).reshape(width, width)
    return (activated, weight_grad)


def solution(mesh):
    split = Mesh(mesh.devices.reshape(SIZES), AXES)
    placed = (P(AXES, None), P(AXES, None, None), P(AXES), P(AXES), P(AXES), P(), P(AXES, None))
    return jax.shard_map(
        body, mesh=split, in_specs=placed, out_specs=(P(AXES, None), P()), check_vma=False
    )
```

```python
import functools

import jax
import jax.numpy as jnp
from jax import lax
from jax.experimental import pallas as pl
from jax.experimental.pallas import tpu as pltpu
from jax.sharding import Mesh, PartitionSpec as P

root_two_pi = 0.7978845608028654
cubic = 0.044715

AXES = ("x", "zl", "c", "yh", "yl", "zh")
SIZES = (4, 2, 2, 4, 2, 4)
NX, NZL, NC, _, _, NZH = SIZES
RING = ("yh", "yl")
NY = 8
ROUNDS = NY // 2
LANES = 128
GROUP = 4
NEAR = ("x", "zl", "c", "yl")
FAR = ("yh", "zh")
NEAR_SIZE = 32
PARTS = (10, 11, 8, 2, 1, 0, 9, 12)
MESSAGES = (
    (0, 0, 3), (1, 1, 5), (0, 0, 2), (1, 1, 6), (0, 1, 6),
    (1, 0, 2), (0, 1, 7), (1, 0, 1), (0, 0, 1), (1, 1, 7),
)


def halves(v):
    high = v.astype(jnp.bfloat16)
    return high, (v - high.astype(jnp.float32)).astype(jnp.bfloat16)


def dot3(a, b, dims):
    ah, al = halves(a)
    bh, bl = halves(b)

    def one(u, v):
        return lax.dot_general(u, v, (dims, ((), ())), preferred_element_type=jnp.float32)

    return one(ah, bh) + (one(al, bh) + one(ah, bl))


def gelu_parts(z):
    inner = root_two_pi * (z + cubic * z * z * z)
    slope_t = jnp.tanh(inner)
    value = 0.5 * z * (1.0 + slope_t)
    slope = 0.5 * (1.0 + slope_t) + 0.5 * z * (1.0 - slope_t * slope_t) * root_two_pi * (
        1.0 + 3.0 * cubic * z * z
    )
    return (value, slope)


def trade(v, axis, way):
    n = lax.axis_size(axis)
    return lax.ppermute(v, axis, [(k, (k + 1 - 2 * ((k + way) % 2)) % n) for k in range(n)])


def ahead(place, axis):
    n = lax.axis_size(axis)
    me = lax.axis_index(axis)
    return lax.rem((1 - 2 * (me % 2)) * (place - me) + n, n)


def swap(v, axes):
    return lax.all_to_all(v, axes, split_axis=0, concat_axis=0, tiled=True)


def share(v, axes):
    return swap(jnp.broadcast_to(v[None], (lax.axis_size(axes),) + v.shape), axes)


def slot_plan(tile_rows, tile_cols, tile_count):
    ids = jnp.arange(tile_rows.shape[0], dtype=jnp.int32)
    far = ahead(tile_rows // NZH, RING)
    part = sum(jnp.where(far == k, PARTS[k], 0) for k in range(NY))
    key = jnp.where(ids < tile_count[0], part // 8, 2)
    row = tile_rows % NZH + part % 8 * NZH
    core = lax.rem(tile_cols % NC + lax.axis_index("c"), NC)
    packed = (ids * 32 + row) * 16 + core * (NX * NZL) + tile_cols // NC
    before = (key[None, :] < key[:, None]) | (
        (key[None, :] == key[:, None]) & (ids[None, :] < ids[:, None])
    )
    place = jnp.sum(before.astype(jnp.int32), axis=1)
    ordered = jnp.sum(jnp.where(place[None, :] == ids[:, None], packed[None, :], 0), axis=1)
    marks = jnp.arange(8, dtype=jnp.int32)
    starts = jnp.sum((key[None, :] < marks[:, None]).astype(jnp.int32), axis=1)
    return ordered, starts


def split_tiles(tiles):
    high = lax.reduce_precision(tiles, exponent_bits=8, mantissa_bits=7)
    return high.astype(jnp.bfloat16), (tiles - high).astype(jnp.bfloat16)


def slot_product(tile_high, tile_low, high, low):
    return jnp.dot(
        jnp.concatenate([tile_high, tile_low, tile_high], axis=1),
        jnp.concatenate([high, high, low], axis=0),
        preferred_element_type=jnp.float32,
    )


def add_products(step, starts_ref, order_ref, left_high, left_low, high, low, out_a_ref, out_b_ref):
    first, last = starts_ref[step], starts_ref[step + 1]
    slots, spare = order_ref.shape[0], out_a_ref.shape[0] - 1
    out_a_ref[...] = jnp.zeros_like(out_a_ref)
    out_b_ref[...] = jnp.zeros_like(out_b_ref)

    @pl.loop(0, (last - first + GROUP - 1) // GROUP)
    def _(group):
        for k in range(GROUP):
            index = first + group * GROUP + k
            packed = order_ref[jnp.minimum(index, slots - 1)]
            row = jnp.where(index < last, packed // 16 % 32, spare)
            slot, block = packed // 512, packed % 16
            value = slot_product(left_high[slot], left_low[slot], high[block], low[block])
            out_a_ref[row] += value[:, :LANES]
            out_b_ref[row] += value[:, LANES:]


def first_kernel(starts_ref, order_ref, left_high, left_low, own_ref, other_ref, out_a_ref, out_b_ref, high, low):
    blocks = own_ref.shape[0]
    for k, source in enumerate((own_ref, other_ref)):
        for b in range(blocks):
            high[k * blocks + b], low[k * blocks + b] = halves(source[b])
    add_products(0, starts_ref, order_ref, left_high, left_low, high, low, out_a_ref, out_b_ref)


def sums_of(step, starts, ordered, left, sources):
    tile = left[0].shape[1]
    rows = NZH * (3, 5)[step] + 1
    shapes = [jax.ShapeDtypeStruct((rows, tile, LANES), jnp.float32)] * 2
    if step == 0:
        shapes += [jax.ShapeDtypeStruct((2 * sources[0].shape[0], tile, 2 * LANES), jnp.bfloat16)] * 2
    smem = pl.BlockSpec(memory_space=pltpu.SMEM)
    vmem = pl.BlockSpec(memory_space=pltpu.VMEM)
    return pl.pallas_call(
        functools.partial(add_products, step) if step else first_kernel,
        out_shape=shapes,
        in_specs=[smem, smem, vmem, vmem, vmem, vmem],
        out_specs=[vmem] * len(shapes),
        compiler_params=pltpu.CompilerParams(vmem_limit_bytes=16 * 1024 * 1024),
        cost_estimate=pl.CostEstimate(flops=10**6, bytes_accessed=2**14, transcendentals=0),
    )(starts, ordered, *left, *sources)


def node_kernel(terms_ref, weight_ref, cot_ref, act_ref, grad_ref):
    agg = (terms_ref[0] + terms_ref[1]) + (terms_ref[2] + terms_ref[3])
    pre = dot3(agg, weight_ref[...], ((1,), (0,)))
    value, slope = gelu_parts(pre)
    act_ref[...] = value
    grad = dot3(agg, cot_ref[...] * slope, ((0,), (0,)))
    rows = grad.shape[0] // NEAR_SIZE
    for r in range(NEAR_SIZE):
        for h in range(2):
            grad_ref[r, h] = grad[rows * r : rows * (r + 1), h * LANES : (h + 1) * LANES]


def node_step(terms, weight, cotangent):
    vmem = pl.BlockSpec(memory_space=pltpu.VMEM)
    return pl.pallas_call(
        node_kernel,
        out_shape=(
            jax.ShapeDtypeStruct(cotangent.shape, jnp.float32),
            jax.ShapeDtypeStruct((NEAR_SIZE, 2, weight.shape[0] // NEAR_SIZE, LANES), jnp.float32),
        ),
        in_specs=[vmem] * 3,
        out_specs=(vmem, vmem),
        compiler_params=pltpu.CompilerParams(vmem_limit_bytes=8 * 1024 * 1024),
    )(terms, weight, cotangent)


def after(value, witness):
    return lax.optimization_barrier((value, witness))[0]


def body(features, adjacency_tiles, tile_rows, tile_cols, tile_count, weight, cotangent):
    ordered, starts = slot_plan(tile_rows, tile_cols, tile_count)
    own = share(features, ("x", "zl"))
    other = lax.ppermute(own, "c", [(0, 1), (1, 0)])
    left = split_tiles(adjacency_tiles)
    *early, high, low = sums_of(0, starts, ordered, left, (own, other))
    late = sums_of(1, after(starts, early[0]), ordered, left, (high, low))

    def chunk(lane, far):
        first = PARTS[far] % 8 * NZH
        return (early, late)[PARTS[far] // 8][lane][first : first + NZH]

    first_a = trade(early[0][: 2 * NZH], RING, 1)
    first_b = trade(early[1][NZH : 3 * NZH], RING, 0)
    came = [first_a[NZH:], first_b[:NZH], first_a[:NZH], first_b[NZH:]]
    made = late[0]
    for k, (lane, way, far) in enumerate(MESSAGES):
        made = chunk(lane, far) + after(came[k], made)
        came.append(trade(made, RING, way))
    part_a = chunk(0, 0) + after(came[10], made)
    part_b = chunk(1, 0) + after(came[11], part_a)
    last_a = part_a + after(came[12], part_b)
    last_b = part_b + after(came[13], last_a)
    terms = swap(jnp.concatenate([last_a, last_b], axis=2), "zh")
    activated, grad = node_step(terms, weight, cotangent)
    grad = jnp.sum(swap(grad, NEAR), axis=0)
    grad = jnp.sum(share(grad, FAR), axis=0)
    grad = share(grad, NEAR)
    width = weight.shape[0]
    weight_grad = grad.swapaxes(1, 2).reshape(width, width)
    return (activated, weight_grad)


def solution(mesh):
    split = Mesh(mesh.devices.reshape(SIZES), AXES)
    placed = (P(AXES, None), P(AXES, None, None), P(AXES), P(AXES), P(AXES), P(), P(AXES, None))
    return jax.shard_map(
        body, mesh=split, in_specs=placed, out_specs=(P(AXES, None), P()), check_vma=False
    )
```

```python
import functools

import jax
import jax.numpy as jnp
from jax import lax
from jax.experimental import pallas as pl
from jax.experimental.pallas import tpu as pltpu
from jax.sharding import Mesh, PartitionSpec as P

root_two_pi = 0.7978845608028654
cubic = 0.044715

AXES = ("x", "zl", "c", "yh", "yl", "zh")
SIZES = (4, 2, 2, 4, 2, 4)
NX, NZL, NC, _, _, NZH = SIZES
RING = ("yh", "yl")
NY = 8
ROUNDS = NY // 2
LANES = 128
GROUP = 4
NEAR = ("x", "zl", "c", "yl")
FAR = ("yh", "zh")
NEAR_SIZE = 32
PARTS = (10, 11, 8, 2, 1, 0, 9, 12)
MESSAGES = (
    (0, 0, 3), (1, 1, 5), (0, 0, 2), (1, 1, 6), (0, 1, 6),
    (1, 0, 2), (0, 1, 7), (1, 0, 1), (0, 0, 1), (1, 1, 7),
)


def halves(v):
    high = v.astype(jnp.bfloat16)
    return high, (v - high.astype(jnp.float32)).astype(jnp.bfloat16)


def dot3(a, b, dims):
    ah, al = halves(a)
    bh, bl = halves(b)

    def one(u, v):
        return lax.dot_general(u, v, (dims, ((), ())), preferred_element_type=jnp.float32)

    return one(ah, bh) + (one(al, bh) + one(ah, bl))


def gelu_parts(z):
    inner = root_two_pi * (z + cubic * z * z * z)
    slope_t = jnp.tanh(inner)
    value = 0.5 * z * (1.0 + slope_t)
    slope = 0.5 * (1.0 + slope_t) + 0.5 * z * (1.0 - slope_t * slope_t) * root_two_pi * (
        1.0 + 3.0 * cubic * z * z
    )
    return (value, slope)


def trade(v, axis, way):
    n = lax.axis_size(axis)
    return lax.ppermute(v, axis, [(k, (k + 1 - 2 * ((k + way) % 2)) % n) for k in range(n)])


def ahead(place, axis):
    n = lax.axis_size(axis)
    me = lax.axis_index(axis)
    return lax.rem((1 - 2 * (me % 2)) * (place - me) + n, n)


def swap(v, axes):
    return lax.all_to_all(v, axes, split_axis=0, concat_axis=0, tiled=True)


def share(v, axes):
    return swap(jnp.broadcast_to(v[None], (lax.axis_size(axes),) + v.shape), axes)


def slot_plan(tile_rows, tile_cols, tile_count):
    ids = jnp.arange(tile_rows.shape[0], dtype=jnp.int32)
    far = ahead(tile_rows // NZH, RING)
    part = sum(jnp.where(far == k, PARTS[k], 0) for k in range(NY))
    key = jnp.where(ids < tile_count[0], part // 8, 2)
    row = tile_rows % NZH + part % 8 * NZH
    core = lax.rem(tile_cols % NC + lax.axis_index("c"), NC)
    packed = (ids * 32 + row) * 16 + core * (NX * NZL) + tile_cols // NC
    before = (key[None, :] < key[:, None]) | (
        (key[None, :] == key[:, None]) & (ids[None, :] < ids[:, None])
    )
    place = jnp.sum(before.astype(jnp.int32), axis=1)
    ordered = jnp.sum(jnp.where(place[None, :] == ids[:, None], packed[None, :], 0), axis=1)
    marks = jnp.arange(8, dtype=jnp.int32)
    starts = jnp.sum((key[None, :] < marks[:, None]).astype(jnp.int32), axis=1)
    return ordered, starts


def split_tiles(tiles):
    high = lax.reduce_precision(tiles, exponent_bits=8, mantissa_bits=7)
    return high.astype(jnp.bfloat16), (tiles - high).astype(jnp.bfloat16)


def slot_product(tile_high, tile_low, high, low):
    return jnp.dot(
        jnp.concatenate([tile_high, tile_low, tile_high], axis=1),
        jnp.concatenate([high, high, low], axis=0),
        preferred_element_type=jnp.float32,
    )


def add_products(step, starts_ref, order_ref, left_high, left_low, high, low, out_a_ref, out_b_ref):
    first, last = starts_ref[step], starts_ref[step + 1]
    slots, spare = order_ref.shape[0], out_a_ref.shape[0] - 1
    out_a_ref[...] = jnp.zeros_like(out_a_ref)
    out_b_ref[...] = jnp.zeros_like(out_b_ref)

    @pl.loop(0, (last - first + GROUP - 1) // GROUP)
    def _(group):
        for k in range(GROUP):
            index = first + group * GROUP + k
            packed = order_ref[jnp.minimum(index, slots - 1)]
            row = jnp.where(index < last, packed // 16 % 32, spare)
            slot, block = packed // 512, packed % 16
            value = slot_product(left_high[slot], left_low[slot], high[block], low[block])
            out_a_ref[row] += value[:, :LANES]
            out_b_ref[row] += value[:, LANES:]


def first_kernel(starts_ref, order_ref, left_high, left_low, own_ref, other_ref, out_a_ref, out_b_ref, high, low):
    blocks = own_ref.shape[0]
    for k, source in enumerate((own_ref, other_ref)):
        for b in range(blocks):
            high[k * blocks + b], low[k * blocks + b] = halves(source[b])
    add_products(0, starts_ref, order_ref, left_high, left_low, high, low, out_a_ref, out_b_ref)


def sums_of(step, starts, ordered, left, sources):
    tile = left[0].shape[1]
    rows = NZH * (3, 5)[step] + 1
    shapes = [jax.ShapeDtypeStruct((rows, tile, LANES), jnp.float32)] * 2
    if step == 0:
        shapes += [jax.ShapeDtypeStruct((2 * sources[0].shape[0], tile, 2 * LANES), jnp.bfloat16)] * 2
    smem = pl.BlockSpec(memory_space=pltpu.SMEM)
    vmem = pl.BlockSpec(memory_space=pltpu.VMEM)
    return pl.pallas_call(
        functools.partial(add_products, step) if step else first_kernel,
        out_shape=shapes,
        in_specs=[smem, smem, vmem, vmem, vmem, vmem],
        out_specs=[vmem] * len(shapes),
        compiler_params=pltpu.CompilerParams(vmem_limit_bytes=16 * 1024 * 1024),
        cost_estimate=pl.CostEstimate(flops=10**6, bytes_accessed=2**14, transcendentals=0),
    )(starts, ordered, *left, *sources)


def node_kernel(terms_ref, weight_ref, cot_ref, act_ref, grad_ref):
    agg = (terms_ref[0] + terms_ref[1]) + (terms_ref[2] + terms_ref[3])
    pre = dot3(agg, weight_ref[...], ((1,), (0,)))
    value, slope = gelu_parts(pre)
    act_ref[...] = value
    grad = dot3(agg, cot_ref[...] * slope, ((0,), (0,)))
    rows = grad.shape[0] // NEAR_SIZE
    for r in range(NEAR_SIZE):
        for h in range(2):
            grad_ref[r, h] = grad[rows * r : rows * (r + 1), h * LANES : (h + 1) * LANES]


def node_step(terms, weight, cotangent):
    vmem = pl.BlockSpec(memory_space=pltpu.VMEM)
    return pl.pallas_call(
        node_kernel,
        out_shape=(
            jax.ShapeDtypeStruct(cotangent.shape, jnp.float32),
            jax.ShapeDtypeStruct((NEAR_SIZE, 2, weight.shape[0] // NEAR_SIZE, LANES), jnp.float32),
        ),
        in_specs=[vmem] * 3,
        out_specs=(vmem, vmem),
        compiler_params=pltpu.CompilerParams(vmem_limit_bytes=8 * 1024 * 1024),
    )(terms, weight, cotangent)


def after(value, witness):
    return lax.optimization_barrier((value, witness))[0]


def body(features, adjacency_tiles, tile_rows, tile_cols, tile_count, weight, cotangent):
    ordered, starts = slot_plan(tile_rows, tile_cols, tile_count)
    own = share(features, ("x", "zl"))
    left = split_tiles(adjacency_tiles)
    ready = lax.optimization_barrier((own, ordered, starts, *left))
    other = lax.ppermute(ready[0], "c", [(0, 1), (1, 0)])
    own, ordered, starts, *left = ready
    *early, high, low = sums_of(0, starts, ordered, left, (own, other))
    late = sums_of(1, after(starts, early[0]), ordered, left, (high, low))

    def chunk(lane, far):
        first = PARTS[far] % 8 * NZH
        return (early, late)[PARTS[far] // 8][lane][first : first + NZH]

    first_a = trade(early[0][: 2 * NZH], RING, 1)
    first_b = trade(early[1][NZH : 3 * NZH], RING, 0)
    came = [first_a[NZH:], first_b[:NZH], first_a[:NZH], first_b[NZH:]]
    made = late[0]
    for k, (lane, way, far) in enumerate(MESSAGES):
        made = chunk(lane, far) + after(came[k], made)
        came.append(trade(made, RING, way))
    part_a = chunk(0, 0) + after(came[10], made)
    part_b = chunk(1, 0) + after(came[11], part_a)
    last_a = part_a + after(came[12], part_b)
    last_b = part_b + after(came[13], last_a)
    terms = swap(jnp.concatenate([last_a, last_b], axis=2), "zh")
    activated, grad = node_step(terms, weight, cotangent)
    grad = jnp.sum(swap(grad, NEAR), axis=0)
    grad = jnp.sum(share(grad, FAR), axis=0)
    grad = share(grad, NEAR)
    width = weight.shape[0]
    weight_grad = grad.swapaxes(1, 2).reshape(width, width)
    return (activated, weight_grad)


def solution(mesh):
    split = Mesh(mesh.devices.reshape(SIZES), AXES)
    placed = (P(AXES, None), P(AXES, None, None), P(AXES), P(AXES), P(AXES), P(), P(AXES, None))
    return jax.shard_map(
        body, mesh=split, in_specs=placed, out_specs=(P(AXES, None), P()), check_vma=False
    )
```

```python
import functools

import jax
import jax.numpy as jnp
from jax import lax
from jax.experimental import pallas as pl
from jax.experimental.pallas import tpu as pltpu
from jax.sharding import Mesh, PartitionSpec as P

root_two_pi = 0.7978845608028654
cubic = 0.044715

AXES = ("x", "zl", "c", "yh", "yl", "zh")
SIZES = (4, 2, 2, 4, 2, 4)
NX, NZL, NC, _, _, NZH = SIZES
RING = ("yh", "yl")
NY = 8
ROUNDS = NY // 2
LANES = 128
GROUP = 4
NEAR = ("x", "zl", "c", "yl")
FAR = ("yh", "zh")
NEAR_SIZE = 32
PARTS = (10, 11, 8, 2, 1, 0, 9, 12)
MESSAGES = (
    (0, 0, 3), (1, 1, 5), (0, 0, 2), (1, 1, 6), (0, 1, 6),
    (1, 0, 2), (0, 1, 7), (1, 0, 1), (0, 0, 1), (1, 1, 7),
)


def halves(v):
    high = v.astype(jnp.bfloat16)
    return high, (v - high.astype(jnp.float32)).astype(jnp.bfloat16)


def dot3(a, b, dims):
    ah, al = halves(a)
    bh, bl = halves(b)

    def one(u, v):
        return lax.dot_general(u, v, (dims, ((), ())), preferred_element_type=jnp.float32)

    return one(ah, bh) + (one(al, bh) + one(ah, bl))


def gelu_parts(z):
    inner = root_two_pi * (z + cubic * z * z * z)
    slope_t = jnp.tanh(inner)
    value = 0.5 * z * (1.0 + slope_t)
    slope = 0.5 * (1.0 + slope_t) + 0.5 * z * (1.0 - slope_t * slope_t) * root_two_pi * (
        1.0 + 3.0 * cubic * z * z
    )
    return (value, slope)


def trade(v, axis, way):
    n = lax.axis_size(axis)
    return lax.ppermute(v, axis, [(k, (k + 1 - 2 * ((k + way) % 2)) % n) for k in range(n)])


def ahead(place, axis):
    n = lax.axis_size(axis)
    me = lax.axis_index(axis)
    return lax.rem((1 - 2 * (me % 2)) * (place - me) + n, n)


def swap(v, axes):
    return lax.all_to_all(v, axes, split_axis=0, concat_axis=0, tiled=True)


def share(v, axes):
    return swap(jnp.broadcast_to(v[None], (lax.axis_size(axes),) + v.shape), axes)


def slot_plan(tile_rows, tile_cols, tile_count):
    ids = jnp.arange(tile_rows.shape[0], dtype=jnp.int32)
    far = ahead(tile_rows // NZH, RING)
    part = sum(jnp.where(far == k, PARTS[k], 0) for k in range(NY))
    key = jnp.where(ids < tile_count[0], part // 8, 2)
    row = tile_rows % NZH + part % 8 * NZH
    core = lax.rem(tile_cols % NC + lax.axis_index("c"), NC)
    packed = (ids * 32 + row) * 16 + core * (NX * NZL) + tile_cols // NC
    before = (key[None, :] < key[:, None]) | (
        (key[None, :] == key[:, None]) & (ids[None, :] < ids[:, None])
    )
    place = jnp.sum(before.astype(jnp.int32), axis=1)
    ordered = jnp.sum(jnp.where(place[None, :] == ids[:, None], packed[None, :], 0), axis=1)
    marks = jnp.arange(8, dtype=jnp.int32)
    starts = jnp.sum((key[None, :] < marks[:, None]).astype(jnp.int32), axis=1)
    return ordered, starts


def split_tiles(tiles):
    high = lax.reduce_precision(tiles, exponent_bits=8, mantissa_bits=7)
    return high.astype(jnp.bfloat16), (tiles - high).astype(jnp.bfloat16)


def slot_product(tile_high, tile_low, high, low):
    return jnp.dot(
        jnp.concatenate([tile_high, tile_low, tile_high], axis=1),
        jnp.concatenate([high, high, low], axis=0),
        preferred_element_type=jnp.float32,
    )


def add_products(step, starts_ref, order_ref, left_high, left_low, high, low, out_a_ref, out_b_ref):
    first, last = starts_ref[step], starts_ref[step + 1]
    slots, spare = order_ref.shape[0], out_a_ref.shape[0] - 1
    out_a_ref[...] = jnp.zeros_like(out_a_ref)
    out_b_ref[...] = jnp.zeros_like(out_b_ref)

    @pl.loop(0, (last - first + GROUP - 1) // GROUP)
    def _(group):
        for k in range(GROUP):
            index = first + group * GROUP + k
            packed = order_ref[jnp.minimum(index, slots - 1)]
            row = jnp.where(index < last, packed // 16 % 32, spare)
            slot, block = packed // 512, packed % 16
            value = slot_product(left_high[slot], left_low[slot], high[block], low[block])
            out_a_ref[row] += value[:, :LANES]
            out_b_ref[row] += value[:, LANES:]


def first_kernel(starts_ref, order_ref, left_high, left_low, own_ref, other_ref, out_a_ref, out_b_ref, high, low):
    blocks = own_ref.shape[0]
    for k, source in enumerate((own_ref, other_ref)):
        for b in range(blocks):
            high[k * blocks + b], low[k * blocks + b] = halves(source[b])
    add_products(0, starts_ref, order_ref, left_high, left_low, high, low, out_a_ref, out_b_ref)


def sums_of(step, starts, ordered, left, sources):
    tile = left[0].shape[1]
    rows = NZH * (3, 5)[step] + 1
    shapes = [jax.ShapeDtypeStruct((rows, tile, LANES), jnp.float32)] * 2
    if step == 0:
        shapes += [jax.ShapeDtypeStruct((2 * sources[0].shape[0], tile, 2 * LANES), jnp.bfloat16)] * 2
    smem = pl.BlockSpec(memory_space=pltpu.SMEM)
    vmem = pl.BlockSpec(memory_space=pltpu.VMEM)
    return pl.pallas_call(
        functools.partial(add_products, step) if step else first_kernel,
        out_shape=shapes,
        in_specs=[smem, smem, vmem, vmem, vmem, vmem],
        out_specs=[vmem] * len(shapes),
        compiler_params=pltpu.CompilerParams(vmem_limit_bytes=16 * 1024 * 1024),
        cost_estimate=pl.CostEstimate(flops=10**6, bytes_accessed=2**14, transcendentals=0),
    )(starts, ordered, *left, *sources)


def node_kernel(terms_ref, weight_ref, cot_ref, act_ref, grad_ref):
    agg = (terms_ref[0] + terms_ref[1]) + (terms_ref[2] + terms_ref[3])
    pre = dot3(agg, weight_ref[...], ((1,), (0,)))
    value, slope = gelu_parts(pre)
    act_ref[...] = value
    grad = dot3(agg, cot_ref[...] * slope, ((0,), (0,)))
    rows = grad.shape[0] // NEAR_SIZE
    for r in range(NEAR_SIZE):
        for h in range(2):
            grad_ref[r, h] = grad[rows * r : rows * (r + 1), h * LANES : (h + 1) * LANES]


def node_step(terms, weight, cotangent):
    vmem = pl.BlockSpec(memory_space=pltpu.VMEM)
    return pl.pallas_call(
        node_kernel,
        out_shape=(
            jax.ShapeDtypeStruct(cotangent.shape, jnp.float32),
            jax.ShapeDtypeStruct((NEAR_SIZE, 2, weight.shape[0] // NEAR_SIZE, LANES), jnp.float32),
        ),
        in_specs=[vmem] * 3,
        out_specs=(vmem, vmem),
        compiler_params=pltpu.CompilerParams(vmem_limit_bytes=8 * 1024 * 1024),
    )(terms, weight, cotangent)


def after(value, witness):
    return lax.optimization_barrier((value, witness))[0]


def body(features, adjacency_tiles, tile_rows, tile_cols, tile_count, weight, cotangent):
    ordered, starts = slot_plan(tile_rows, tile_cols, tile_count)
    own = share(features, ("x", "zl"))
    left = split_tiles(adjacency_tiles)
    other = lax.ppermute(lax.optimization_barrier((own, left[0], ordered))[0], "c", [(0, 1), (1, 0)])
    *early, high, low = sums_of(0, starts, ordered, left, (own, other))
    late = sums_of(1, after(starts, early[0]), ordered, left, (high, low))

    def chunk(lane, far):
        first = PARTS[far] % 8 * NZH
        return (early, late)[PARTS[far] // 8][lane][first : first + NZH]

    first_a = trade(early[0][: 2 * NZH], RING, 1)
    first_b = trade(early[1][NZH : 3 * NZH], RING, 0)
    came = [first_a[NZH:], first_b[:NZH], first_a[:NZH], first_b[NZH:]]
    made = late[0]
    for k, (lane, way, far) in enumerate(MESSAGES):
        made = chunk(lane, far) + after(came[k], made)
        came.append(trade(made, RING, way))
    part_a = chunk(0, 0) + after(came[10], made)
    part_b = chunk(1, 0) + after(came[11], part_a)
    last_a = part_a + after(came[12], part_b)
    last_b = part_b + after(came[13], last_a)
    terms = swap(jnp.concatenate([last_a, last_b], axis=2), "zh")
    activated, grad = node_step(terms, weight, cotangent)
    grad = jnp.sum(swap(grad, NEAR), axis=0)
    grad = jnp.sum(share(grad, FAR), axis=0)
    grad = share(grad, NEAR)
    width = weight.shape[0]
    weight_grad = grad.swapaxes(1, 2).reshape(width, width)
    return (activated, weight_grad)


def solution(mesh):
    split = Mesh(mesh.devices.reshape(SIZES), AXES)
    placed = (P(AXES, None), P(AXES, None, None), P(AXES), P(AXES), P(AXES), P(), P(AXES, None))
    return jax.shard_map(
        body, mesh=split, in_specs=placed, out_specs=(P(AXES, None), P()), check_vma=False
    )
```
